1024 devices in a mesh: clip: 16 (over y, z_hi), seq: 64 (over x, z_lo, core).
Axes of the slice: x: 4, y: 4, z: 32 (z_hi: 4, z_lo: 8; z = z_hi * 8 + z_lo), core: 2. Of those that a mesh axis runs over, the one named last changes fastest.
Arguments:
- hidden_activation: bfloat16 [16, 8192, 1024], P('clip', 'seq'), may hold values from -6 to 6
- projection_weight: bfloat16 [1024, 1536], replicated, may hold values from -0.1875 to 0.1875
- projection_bias: float32 [1536], replicated, may hold values from -6 to 6
- patch_feats: bfloat16 [16, 16384, 1536], P('clip', 'seq'), may hold values from -6 to 6
- pool_slot: int32 [16, 16384], P('clip', 'seq'), may hold values from 0 to 1, as said below
- token_order: int32 [16, 8192], P('clip', 'seq'), may hold values from 0 to 127, as said below
- cos_cotangent: float32 [16, 8192], P('clip', 'seq'), may hold values from -24 to 24
Outputs:
- cos_sim: float32 [16, 8192], P('clip', 'seq')
- weight_grad: float32 [1024, 1536], P('clip')
- bias_grad: float32 [1536], P('clip')
The draws below stay inside these ranges and needn't reach their ends.
Inputs may be any that keep to these rules, and one draw needn't show every extreme that they name: `pool_slot`: patches come in aligned blocks of 4; each block names every slot 0 to 1 at least once. `token_order`: each aligned block of 128 entries is a permutation of 0 to 127.
All inputs are finite; a program needn't handle non-finite values.
Results may differ from the reference program's by a relative error of at most 0.025.
Values may be sent and summed in bfloat16 or wider, within the bound.
No kernel may reach another device: no remote copies, remote signals or barrier semaphores. Data moves between devices by JAX's collectives and lax.ppermute only.
A program may use at most 64 MiB of HBM per device.

```python
import jax
import jax.numpy as jnp
from jax import lax

PH = 1024
DD = 1536
LAT_DEV = 128
SEQ_SHARDS = 64
SLOTS = 2
PATCH_BLOCK = 4
CLIPS = 16
LAT = 8192
PATCH = 16384
TOTAL_TOK = 131072


def draw_pool_slot(key, part):
    key = jax.random.fold_in(key, 11)
    first_key, second_key = jax.random.split(key)
    blocks = CLIPS * PATCH // PATCH_BLOCK
    covered = jnp.tile(jnp.arange(SLOTS, dtype=jnp.int32)[None, :], (blocks, 1))
    extra = jax.random.randint(first_key, (blocks, PATCH_BLOCK - SLOTS), 0, SLOTS, dtype=jnp.int32)
    base_slots = jnp.concatenate([covered, extra], axis=1)
    scores = jax.random.randint(second_key, (blocks, PATCH_BLOCK), 0, 1 << 20, dtype=jnp.int32)
    scores = scores * PATCH_BLOCK + jnp.arange(PATCH_BLOCK, dtype=jnp.int32)[None, :]
    ordering = jnp.argsort(scores, axis=1, stable=True)
    return jnp.take_along_axis(base_slots, ordering, axis=1).reshape(CLIPS, PATCH).astype(jnp.int32)


def draw_token_order(key, part):
    key = jax.random.fold_in(key, 23)
    blocks = CLIPS * LAT // LAT_DEV
    scores = jax.random.randint(key, (blocks, LAT_DEV), 0, 1 << 16, dtype=jnp.int32)
    scores = scores * LAT_DEV + jnp.arange(LAT_DEV, dtype=jnp.int32)[None, :]
    ordering = jnp.argsort(scores, axis=1, stable=True)
    return ordering.reshape(CLIPS, LAT).astype(jnp.int32)


def steps_of(rng, extent, shards, smallest, high):
    level, own = 1.0, jax.random.fold_in(rng, 6)
    for axis_at, blocks in shards:
        steps = jnp.exp(jax.random.uniform(jax.random.fold_in(own, axis_at), (blocks,), jnp.float32, smallest / len(shards), high / len(shards)))
        level = level * jnp.repeat(steps, extent[axis_at] // blocks).reshape([-1 if axis == axis_at else 1 for axis in range(len(extent))])
    return level


def noise(own_key, extent, spread, most, cuts=(), held_as=jnp.bfloat16):
    result = jax.random.normal(own_key, extent, jnp.float32) * spread
    if len(cuts) > 0:
        result = steps_of(own_key, extent, cuts, -0.22, 0.18) * result
    return jnp.clip(result, min=-most, max=most).astype(held_as)


def setup_inputs(seed: int = 0) -> dict:
    splits = jax.random.split(jax.random.key(seed), 8)
    hidden_activation = noise(splits[0], (CLIPS, LAT, PH), 1.0, 6.0, ((0, 16), (1, 64)))
    projection_weight = noise(splits[1], (PH, DD), PH ** -0.5, 0.1875)
    projection_bias = noise(splits[2], (DD,), 1.0, 6.0, (), jnp.float32)
    patch_feats = noise(splits[3], (CLIPS, PATCH, DD), 1.0, 6.0, ((0, 16), (1, 64)))
    pool_slot = draw_pool_slot(jax.random.fold_in(splits[7], 71), 0)
    token_order = draw_token_order(jax.random.fold_in(splits[7], 71), 0)
    cos_cotangent = noise(splits[6], (CLIPS, LAT), (1500 * TOTAL_TOK ** -0.5), 24.0, ((0, 16), (1, 64)), jnp.float32)
    return {"hidden_activation": hidden_activation, "projection_weight": projection_weight, "projection_bias": projection_bias, "patch_feats": patch_feats, "pool_slot": pool_slot, "token_order": token_order, "cos_cotangent": cos_cotangent}


def pool_clip(patches, slot_ids):
    grouped = patches.reshape(SEQ_SHARDS, SEQ_SHARDS, PATCH_BLOCK, DD).astype(jnp.float32)
    slot_grid = slot_ids.reshape(SEQ_SHARDS, SEQ_SHARDS, PATCH_BLOCK)
    levels = jnp.arange(SLOTS, dtype=jnp.int32)
    onehot = (slot_grid[:, :, None, :] == levels[None, None, :, None]).astype(jnp.float32)
    totals = jnp.einsum('sjlp,sjpd->jsld', onehot, grouped)
    counts = jnp.transpose(lax.optimization_barrier(jnp.sum(onehot, axis=3)), (1, 0, 2))
    pooled = (totals / counts[:, :, :, None]).astype(jnp.bfloat16)
    return pooled.reshape(SEQ_SHARDS, LAT_DEV, DD)

def rounded(values):
    return lax.optimization_barrier(values.astype(jnp.bfloat16)).astype(jnp.float32)

def reference(hidden_activation, projection_weight, projection_bias, patch_feats, pool_slot, token_order, cos_cotangent):

    def per_clip(totals_in, pieces):
        hidden, patches, slot_ids, ordering, cotangent = pieces
        pooled = pool_clip(patches, slot_ids)
        picks = ordering.reshape(SEQ_SHARDS, LAT_DEV).astype(jnp.int32)
        target = jnp.take_along_axis(pooled, picks[:, :, None], axis=1).reshape(LAT, DD)
        target = target.astype(jnp.float32)
        projected_rows = jnp.dot(hidden, projection_weight, preferred_element_type=jnp.float32) + projection_bias
        inv_proj = lax.rsqrt(lax.optimization_barrier(jnp.sum(projected_rows * projected_rows, axis=1)) + 1e-06)
        inv_target = lax.rsqrt(lax.optimization_barrier(jnp.sum(target * target, axis=1)) + 1e-06)
        cosine = lax.optimization_barrier(jnp.sum(projected_rows * target, axis=1)) * inv_proj * inv_target
        gradient_rows_local = cotangent[:, None] * (target * (inv_proj * inv_target)[:, None] - (cosine * inv_proj * inv_proj)[:, None] * projected_rows)
        gradient_rows_local = gradient_rows_local.astype(jnp.bfloat16)

        def per_shard(running, device_portion):
            transformer_rows, portion_gradients = device_portion
            weight_portion = lax.dot_general(transformer_rows, portion_gradients, (((0,), (0,)), ((), ())), preferred_element_type=jnp.float32)
            bias_part = lax.optimization_barrier(jnp.sum(portion_gradients.astype(jnp.float32), axis=0))
            return ((running[0] + rounded(weight_portion), running[1] + rounded(bias_part)), None)
        totals_out, unused = lax.scan(per_shard, totals_in, (hidden.reshape(SEQ_SHARDS, LAT_DEV, PH), gradient_rows_local.reshape(SEQ_SHARDS, LAT_DEV, DD)))
        return (totals_out, cosine)
    start = (jnp.zeros((PH, DD), jnp.float32), jnp.zeros((DD,), jnp.float32))
    totals, cos_sim = lax.scan(per_clip, start, (hidden_activation, patch_feats, pool_slot, token_order, cos_cotangent))
    return (cos_sim, totals[0], totals[1])
```

```python
import jax
import jax.numpy as jnp
from jax import lax
from jax.sharding import Mesh, PartitionSpec as P

BF = jnp.bfloat16
F32 = jnp.float32
LANES = 128


def split_terms(values, terms):
    parts = []
    for _ in range(terms - 1):
        head = lax.reduce_precision(values, 8, 7)
        parts.append(head.astype(BF))
        values = values - head
    parts.append(values.astype(BF))
    return parts


def join_terms(parts):
    total = parts[-1].astype(F32)
    for part in parts[-2::-1]:
        total = total + part.astype(F32)
    return total


def local(hidden, weight, bias, patches, slots, order, cotangent):
    y_n, h_n, x_n, l_n, c_n = (lax.axis_size(a) for a in ("y", "h", "x", "l", "c"))
    hidden, patches = hidden[0], patches[0]
    slots, order, cotangent = slots[0], order[0], cotangent[0]
    tokens, units = hidden.shape
    width = weight.shape[1]
    patch_count = patches.shape[0]
    near = x_n * l_n
    per = tokens // near
    shards = near * c_n
    two = tokens // shards
    block = patch_count // shards
    half = width // c_n
    rows = units // (y_n * h_n)
    own = rows // near
    core = lax.axis_index("c")

    pick = order[None, :] == jnp.arange(tokens, dtype=jnp.int32)[:, None]
    sent_rows = jnp.dot(pick.astype(BF), hidden, preferred_element_type=F32).astype(BF)
    sent_cot = jnp.sum(jnp.where(pick, cotangent[None, :], 0.0), axis=1)
    cot_cols = jnp.stack(split_terms(sent_cot, 3), axis=1)
    cot_cols = jnp.pad(cot_cols, ((0, 0), (0, LANES - 3)))
    sent = jnp.concatenate([sent_rows, cot_cols], axis=1).reshape(near, per, units + LANES)
    moved = lax.all_to_all(sent, ("x", "l"), 0, 0, tiled=True)

    at = jnp.arange(tokens, dtype=jnp.int32)
    src_core, src_chip, level = at // (near * two), (at // two) % near, at % two
    src = src_chip * c_n + src_core
    q = jnp.arange(patch_count, dtype=jnp.int32)
    match = (q[None, :] // block == src[:, None]) & (slots[None, :] == level[:, None])
    totals = jnp.dot(match.astype(BF), patches, preferred_element_type=F32)
    counts = jnp.sum(match.astype(F32), axis=1)
    pooled = (totals / counts[:, None]).astype(BF)
    target = lax.all_gather(pooled, "c", axis=0, tiled=True)
    target = target.reshape(c_n, shards, two, width).transpose(1, 0, 2, 3)
    target = target.reshape(c_n * tokens, width).astype(F32)

    both = lax.all_gather(moved, "c", axis=0, tiled=True).reshape(c_n * tokens, units + LANES)
    acts = both[:, :units]
    cot = join_terms([both[:, units + k] for k in range(3)])
    projected = jnp.dot(acts, weight, preferred_element_type=F32) + bias
    inv_proj = lax.rsqrt(jnp.sum(projected * projected, axis=1) + 1e-06)
    inv_target = lax.rsqrt(jnp.sum(target * target, axis=1) + 1e-06)
    cosine = jnp.sum(projected * target, axis=1) * inv_proj * inv_target
    grads = cot[:, None] * (
        target * (inv_proj * inv_target)[:, None] - (cosine * inv_proj * inv_proj)[:, None] * projected
    )
    grads = grads.astype(BF)
    grads_half = lax.dynamic_slice_in_dim(grads, core * half, half, axis=1)
    part = lax.dot_general(acts, grads_half, (((0,), (0,)), ((), ())), preferred_element_type=F32)
    part = part.astype(BF).reshape(y_n, h_n, x_n, rows // x_n, half).transpose(0, 2, 1, 3, 4)
    part = part.reshape(y_n * x_n, h_n * rows // x_n, half)
    cols = width // (y_n * h_n)
    bias_part = jnp.sum(grads.astype(F32), axis=0).astype(BF).reshape(y_n * x_n, 1, cols)
    bias_part = jnp.pad(bias_part, ((0, 0), (0, 7), (0, half - cols)))
    part = jnp.concatenate([part, bias_part], axis=1)

    part = lax.all_to_all(part, ("y", "x"), 0, 0, tiled=True)
    plane = jnp.sum(part.astype(F32), axis=0)
    lines = own * half // LANES
    plane_w = plane[:-8].astype(BF).reshape(h_n * l_n, lines, LANES)
    plane_b = jnp.pad(jnp.stack(split_terms(plane[-8, :cols], 2)), ((0, 14 - lines), (0, LANES - cols)))
    plane_b = jnp.broadcast_to(plane_b, (h_n * l_n, 16 - lines, LANES))
    part = jnp.concatenate([plane_w, plane_b], axis=1)
    part = lax.all_to_all(part, ("h", "l"), 0, 0, tiled=True).astype(F32)
    full_w = jnp.sum(part[:, :lines], axis=0).astype(BF)
    full_b = jnp.sum(part[:, lines] + part[:, lines + 1], axis=0)

    back = lax.dynamic_slice_in_dim(cosine.reshape(c_n, near, per), core, 1, axis=0)[0]
    back = jnp.pad(jnp.stack(split_terms(back, 2), axis=1), ((0, 0), (0, 0), (0, LANES - per)))
    ahead = jnp.concatenate([full_w, jnp.stack(split_terms(full_b, 2))], axis=0)
    ahead = jnp.broadcast_to(ahead, (near, lines + 2, LANES))
    part = lax.all_to_all(jnp.concatenate([ahead, back], axis=1), ("x", "l"), 0, 0, tiled=True)
    block_w = part[:, :lines].reshape(rows, half)
    weight_grad = lax.all_gather(block_w, "c", axis=1, tiled=True).astype(F32)
    mine = lax.dynamic_slice_in_dim(part, lax.axis_index("h") * l_n, 1, axis=0)[0]
    bias_grad = (mine[lines].astype(F32) + mine[lines + 1].astype(F32))[:cols]
    by_slot = (part[:, lines + 2].astype(F32) + part[:, lines + 3].astype(F32))[:, :per].reshape(tokens)
    cos_out = jnp.sum(jnp.where(pick, by_slot[:, None], 0.0), axis=0)
    return cos_out[None, :], weight_grad, bias_grad


def solution(mesh, sizes=(4, 4, 4, 8, 2)):
    fine = Mesh(mesh.devices.reshape(sizes), ("y", "h", "x", "l", "c"))
    clip, seq = ("y", "h"), ("x", "l", "c")
    placed = (
        P(clip, seq, None),
        P(),
        P(),
        P(clip, seq, None),
        P(clip, seq),
        P(clip, seq),
        P(clip, seq),
    )
    return jax.shard_map(
        local,
        mesh=fine,
        in_specs=placed,
        out_specs=(P(clip, seq), P(clip, None), P(clip)),
        check_vma=False,
    )
```

```python
import functools

import jax
import jax.numpy as jnp
from jax import lax
from jax.experimental import pallas as pl
from jax.experimental.pallas import tpu as pltpu
from jax.sharding import Mesh, PartitionSpec as P

BF = jnp.bfloat16
F32 = jnp.float32
I32 = jnp.int32
LANES = 128
TAIL = 16
LINE_ROWS = 2
VMEM = pl.BlockSpec(memory_space=pltpu.VMEM)
SMEM = pl.BlockSpec(memory_space=pltpu.SMEM)


def iota(shape, axis):
    return lax.broadcasted_iota(I32, shape, axis)


def split_two(values):
    head = values.astype(BF)
    return head, (values - head.astype(F32)).astype(BF)


def call(body, outs, ins, scratch=(), limit=40):
    return pl.pallas_call(
        body,
        out_shape=outs,
        in_specs=ins,
        out_specs=jax.tree.map(lambda _: VMEM, outs),
        scratch_shapes=list(scratch),
        compiler_params=pltpu.CompilerParams(vmem_limit_bytes=limit << 20),
    )


def send_kernel(hidden_ref, order_ref, cot_ref, out_ref):
    tokens, units = hidden_ref.shape
    pick = order_ref[...] == iota((tokens, tokens), 0)
    rows = jnp.dot(
        jnp.where(pick, 1.0, 0.0).astype(BF), hidden_ref[...], preferred_element_type=F32
    )
    out_ref[:, :units] = rows.astype(BF)
    cot = jnp.sum(jnp.where(pick, cot_ref[...], 0.0), axis=1, keepdims=True)
    high = cot.astype(BF).astype(F32)
    rest = cot - high
    middle = rest.astype(BF).astype(F32)
    low = rest - middle
    lane = iota((tokens, LANES), 1)
    cols = jnp.where(lane == 0, high, jnp.where(lane == 1, middle, jnp.where(lane == 2, low, 0.0)))
    out_ref[:, units:] = cols.astype(BF)


def middle_kernel(
    dims, core_ref, both_ref, pooled_ref, weight_ref, bias_ref, part_ref, back_ref, proj, target, grads
):
    y_n, h_n, x_n, l_n, c_n, two = dims
    near, per = x_n * l_n, c_n * two
    tokens, units = both_ref.shape[0], both_ref.shape[1] - LANES
    width = weight_ref.shape[1]
    half = width // c_n
    single = tokens // c_n
    core = core_ref[0]
    row = iota((tokens, tokens), 0)
    wanted = (
        (row // two) % c_n * single + row // single * (near * two) + row // per % near * two + row % two
    )
    turn = jnp.where(wanted == iota((tokens, tokens), 1), 1.0, 0.0).astype(BF)
    acts = both_ref[:, :units]
    step = 256
    s_pp = jnp.zeros((tokens, 1), F32)
    s_tt = jnp.zeros((tokens, 1), F32)
    s_pt = jnp.zeros((tokens, 1), F32)
    for at in range(0, width, step):
        cut = slice(at, at + step)
        p = jnp.dot(acts, weight_ref[:, cut], preferred_element_type=F32) + bias_ref[:, cut]
        t = jnp.dot(turn, pooled_ref[:, cut], preferred_element_type=F32)
        proj[:, cut] = p
        target[:, cut] = t
        s_pp = s_pp + jnp.sum(p * p, axis=1, keepdims=True)
        s_tt = s_tt + jnp.sum(t * t, axis=1, keepdims=True)
        s_pt = s_pt + jnp.sum(p * t, axis=1, keepdims=True)
    inv_proj = lax.rsqrt(s_pp + 1e-06)
    inv_target = lax.rsqrt(s_tt + 1e-06)
    cosine = s_pt * inv_proj * inv_target
    terms = both_ref[:, units:].astype(F32)
    cot = (terms[:, 2:3] + terms[:, 1:2]) + terms[:, 0:1]
    scale_t = inv_proj * inv_target
    scale_p = cosine * inv_proj * inv_proj
    y_blocks = width // y_n // LANES
    tail_row = iota((TAIL, step), 0)
    main = part_ref.shape[1] - TAIL
    for at in range(0, width, step):
        g = cot * (target[:, at : at + step] * scale_t - scale_p * proj[:, at : at + step])
        g = g.astype(BF)
        inside = at % half
        grads[at // half, :, inside : inside + step] = g
        total = jnp.sum(g.astype(F32), axis=0, keepdims=True)
        high = total.astype(BF).astype(F32)
        tail = jnp.where(tail_row == 0, high, jnp.where(tail_row == 1, total - high, 0.0)).astype(BF)
        for k in range(step // LANES):
            block = at // LANES + k
            piece = block // y_blocks * x_n + block % y_blocks
            part_ref[piece, main:, :] = tail[:, k * LANES : (k + 1) * LANES]
    for y in range(y_n):
        for x in range(y_blocks, x_n):
            part_ref[y * x_n + x, main:, :] = jnp.zeros((TAIL, LANES), BF)
    lane = iota((tokens, LANES), 1)
    high, low = split_two(cosine)
    spot = iota((tokens, LANES), 0) % per == lane
    owner = iota((near, tokens), 1) - core * single
    gather = jnp.where((owner >= 0) & (owner < single) & (owner // per == iota((near, tokens), 0)), 1.0, 0.0)
    gather = gather.astype(BF)
    back = jnp.zeros((near, LANES), F32)
    for term in (high, low):
        spread = jnp.where(spot, term.astype(F32), 0.0).astype(BF)
        back = back + jnp.dot(gather, spread, preferred_element_type=F32)
    back_ref[...] = back
    rows = units // y_n
    chunk = rows // h_n // x_n
    mine = grads[core]
    for y in range(y_n):
        product = lax.dot_general(
            acts[:, y * rows : (y + 1) * rows], mine, (((0,), (0,)), ((), ())), preferred_element_type=F32
        ).astype(BF)
        for h in range(h_n):
            for x in range(x_n):
                start = (h * x_n + x) * chunk
                for k in range(half // LANES):
                    to = (k * h_n + h) * chunk
                    part_ref[y * x_n + x, to : to + chunk, :] = product[
                        start : start + chunk, k * LANES : (k + 1) * LANES
                    ]


def plane_kernel(dims, part_ref, out_ref, spread):
    y_n, h_n, x_n, l_n, c_n, two = dims
    count, total_rows = part_ref.shape[0], part_ref.shape[1]
    main = total_rows - TAIL
    spread[...] = jnp.zeros_like(spread)
    group = out_ref.shape[0] // (h_n * l_n)
    lines = main // (h_n * l_n)

    def summed(start, size):
        total = part_ref[0, start : start + size, :].astype(F32)
        for p in range(1, count):
            total = total + part_ref[p, start : start + size, :].astype(F32)
        return total

    pair = lines // LINE_ROWS
    size = h_n * LINE_ROWS * l_n
    for k in range(pair):
        total = summed(k * size, size)
        for h in range(h_n):
            for r in range(LINE_ROWS):
                at = (h * LINE_ROWS + r) * l_n
                spread[pl.ds(h * l_n * group + k * LINE_ROWS + r, l_n, stride=group), :] = total[at : at + l_n]
    tail = summed(main, TAIL)
    bias = tail[0:1] + tail[1:2]
    high = bias.astype(BF).astype(F32)
    for r, value in enumerate((high, bias - high)):
        full = jnp.broadcast_to(value, (h_n * l_n, LANES))
        spread[pl.ds(lines + r, h_n * l_n, stride=group), :] = full
    out_ref[...] = spread[...].astype(BF)


def line_kernel(lines, part_ref, back_ref, out_ref):
    total = part_ref[0].astype(F32)
    for p in range(1, part_ref.shape[0]):
        total = total + part_ref[p].astype(F32)
    group = total.shape[0]
    row = iota((group, LANES), 0)
    bias = total[lines : lines + 1] + total[lines + 1 : lines + 2]
    high = bias.astype(BF).astype(F32)
    total = jnp.where(row == lines, high, jnp.where(row == lines + 1, bias - high, total))
    for p in range(out_ref.shape[0]):
        value = back_ref[p : p + 1, :]
        head = value.astype(BF).astype(F32)
        tile = jnp.where(row == group - 2, head, jnp.where(row == group - 1, value - head, total))
        out_ref[p] = tile.astype(BF)


def unpack_kernel(dims, high_ref, own_ref, both_ref, order_ref, cos_ref, weight_ref, bias_ref, wide, narrow):
    y_n, h_n, x_n, l_n, c_n, two = dims
    near, per = x_n * l_n, c_n * two
    group = own_ref.shape[0] // near
    wide[...] = both_ref[...].astype(F32)
    narrow[...] = own_ref[...].astype(F32)
    half = weight_ref.shape[1] // c_n
    pairs = half // LANES
    lines = pairs * LINE_ROWS
    for c in range(c_n):
        for x in range(x_n):
            for k in range(pairs):
                for r in range(LINE_ROWS):
                    start = (c * near + x * l_n) * group + k * LINE_ROWS + r
                    to = (x * LINE_ROWS + r) * l_n
                    at = c * half + k * LANES
                    weight_ref[to : to + l_n, at : at + LANES] = wide[pl.ds(start, l_n, stride=group), :]
    cosines = narrow[pl.ds(group - 2, near, stride=group), :] + narrow[pl.ds(group - 1, near, stride=group), :]
    order = order_ref[...]
    tokens = order.shape[1]
    base = iota((near, tokens), 0) * per
    total = jnp.zeros((near, tokens), F32)
    for i in range(per):
        total = total + jnp.where(order == base + i, cosines[:, i : i + 1], 0.0)
    cos_ref[...] = jnp.sum(total, axis=0, keepdims=True)
    cols = bias_ref.shape[1]
    blocks = cols * h_n // LANES
    offset = high_ref[0] * cols
    out = jnp.zeros((8, cols), F32)
    for b in range(blocks):
        start = b * l_n * group + lines
        pick = iota((LANES, cols), 0) + b * LANES == iota((LANES, cols), 1) + offset
        pick = jnp.where(pick, 1.0, 0.0).astype(BF)
        for r in range(2):
            term = jnp.broadcast_to(narrow[start + r : start + r + 1, :], (8, LANES)).astype(BF)
            out = out + jnp.dot(term, pick, preferred_element_type=F32)
    bias_ref[...] = out[0:1]


def local(hidden, weight, bias, patches, slots, order, cotangent):
    y_n, h_n, x_n, l_n, c_n = (lax.axis_size(a) for a in ("y", "h", "x", "l", "c"))
    patches, slots = patches[0], slots[0]
    tokens, units = hidden.shape[1:]
    width = weight.shape[1]
    patch_count = patches.shape[0]
    near = x_n * l_n
    per = tokens // near
    shards = near * c_n
    two = tokens // shards
    block = patch_count // shards
    half = width // c_n
    dims = (y_n, h_n, x_n, l_n, c_n, two)
    shape = jax.ShapeDtypeStruct
    core = lax.axis_index("c").astype(I32)[None]
    high = lax.axis_index("h").astype(I32)[None]

    sent = call(send_kernel, shape((tokens, units + LANES), BF), [VMEM] * 3)(hidden[0], order, cotangent)
    moved = lax.all_to_all(sent.reshape(near, per, units + LANES), ("x", "l"), 0, 0, tiled=True)

    at = jnp.arange(tokens, dtype=I32)
    src_core, src_chip, level = at // (near * two), (at // two) % near, at % two
    src = src_chip * c_n + src_core
    q = jnp.arange(patch_count, dtype=I32)
    match = (q[None, :] // block == src[:, None]) & (slots[None, :] == level[:, None])
    totals = jnp.dot(match.astype(BF), patches, preferred_element_type=F32)
    counts = jnp.sum(match.astype(F32), axis=1)
    pooled = lax.all_gather((totals / counts[:, None]).astype(BF), "c", axis=0, tiled=True)

    both = lax.all_gather(moved.reshape(tokens, units + LANES), "c", axis=0, tiled=True)
    rows = units // (y_n * x_n)
    lines = half // LANES * LINE_ROWS
    part, back = call(
        functools.partial(middle_kernel, dims),
        (
            shape((y_n * x_n, rows * half // LANES + TAIL, LANES), BF),
            shape((near, LANES), F32),
        ),
        [SMEM] + [VMEM] * 4,
        [
            pltpu.VMEM((c_n * tokens, width), F32),
            pltpu.VMEM((c_n * tokens, width), F32),
            pltpu.VMEM((c_n, c_n * tokens, half), BF),
        ],
    )(core, both, pooled, weight, bias[None, :])

    part = lax.all_to_all(part, ("y", "x"), 0, 0, tiled=True)
    spots = h_n * l_n
    part = call(
        functools.partial(plane_kernel, dims),
        shape((spots * TAIL, LANES), BF),
        [VMEM],
        [pltpu.VMEM((spots * TAIL, LANES), F32)],
    )(part)
    part, back = lax.optimization_barrier((part, back))
    part = lax.all_to_all(part.reshape(spots, TAIL, LANES), ("h", "l"), 0, 0, tiled=True)
    part = call(functools.partial(line_kernel, lines), shape((near, TAIL, LANES), BF), [VMEM] * 2)(part, back)
    part = lax.all_to_all(part, ("x", "l"), 0, 0, tiled=True).reshape(near * TAIL, LANES)
    wide = lax.all_gather(part, "c", axis=0, tiled=True)
    cos_sim, weight_grad, bias_grad = call(
        functools.partial(unpack_kernel, dims),
        (
            shape((1, tokens), F32),
            shape((units // (y_n * h_n), width), F32),
            shape((1, width // (y_n * h_n)), F32),
        ),
        [SMEM] + [VMEM] * 3,
        [pltpu.VMEM((c_n * near * TAIL, LANES), F32), pltpu.VMEM((near * TAIL, LANES), F32)],
    )(high, part, wide, order)
    return cos_sim, weight_grad, bias_grad[0]


def solution(mesh, sizes=(4, 4, 4, 8, 2)):
    fine = Mesh(mesh.devices.reshape(sizes), ("y", "h", "x", "l", "c"))
    clip, seq = ("y", "h"), ("x", "l", "c")
    placed = (
        P(clip, seq, None),
        P(),
        P(),
        P(clip, seq, None),
        P(clip, seq),
        P(clip, seq),
        P(clip, seq),
    )
    return jax.shard_map(
        local,
        mesh=fine,
        in_specs=placed,
        out_specs=(P(clip, seq), P(clip, None), P(clip)),
        check_vma=False,
    )
```

```python
import functools

import jax
import jax.numpy as jnp
from jax import lax
from jax.experimental import pallas as pl
from jax.experimental.pallas import tpu as pltpu
from jax.sharding import Mesh, PartitionSpec as P

BF = jnp.bfloat16
F32 = jnp.float32
I32 = jnp.int32
LANES = 128
TAIL = 16
LINE_ROWS = 2
VMEM = pl.BlockSpec(memory_space=pltpu.VMEM)
SMEM = pl.BlockSpec(memory_space=pltpu.SMEM)


def iota(shape, axis):
    return lax.broadcasted_iota(I32, shape, axis)


def split_two(values):
    head = values.astype(BF)
    return head, (values - head.astype(F32)).astype(BF)


def call(body, outs, ins, scratch=(), limit=40):
    return pl.pallas_call(
        body,
        out_shape=outs,
        in_specs=ins,
        out_specs=jax.tree.map(lambda _: VMEM, outs),
        scratch_shapes=list(scratch),
        compiler_params=pltpu.CompilerParams(vmem_limit_bytes=limit << 20),
    )


def send_kernel(hidden_ref, order_ref, cot_ref, out_ref):
    tokens, units = hidden_ref.shape
    pieces, per = out_ref.shape[:2]
    pick = order_ref[...] == iota((tokens, tokens), 0)
    rows = jnp.dot(
        jnp.where(pick, 1.0, 0.0).astype(BF), hidden_ref[...], preferred_element_type=F32
    )
    cot = jnp.sum(jnp.where(pick, cot_ref[...], 0.0), axis=1, keepdims=True)
    high = cot.astype(BF).astype(F32)
    rest = cot - high
    middle = rest.astype(BF).astype(F32)
    low = rest - middle
    lane = iota((tokens, LANES), 1)
    cols = jnp.where(lane == 0, high, jnp.where(lane == 1, middle, jnp.where(lane == 2, low, 0.0)))
    for p in range(pieces):
        at = slice(p * per, (p + 1) * per)
        out_ref[p] = jnp.concatenate([rows[at], cols[at]], axis=1).astype(BF)


def pool_kernel(dims, patch_ref, slot_ref, weight_ref, pooled_ref, near_ref, sem):
    y_n, h_n, x_n, l_n, c_n, two = dims
    fetch = pltpu.make_async_copy(weight_ref, near_ref, sem)
    fetch.start()
    tokens, patches = pooled_ref.shape[0], patch_ref.shape[0]
    shape = (tokens, patches)
    row = iota(shape, 0)
    near = x_n * l_n
    src = row // two % near * c_n + row // (near * two)
    match = (iota(shape, 1) // (patches // (near * c_n)) == src) & (slot_ref[...] == row % two)
    match = jnp.where(match, 1.0, 0.0)
    counts = jnp.sum(match, axis=1, keepdims=True)
    totals = jnp.dot(match.astype(BF), patch_ref[...], preferred_element_type=F32)
    pooled_ref[...] = (totals / counts).astype(BF)
    fetch.wait()


def middle_kernel(
    dims, core_ref, high_ref, both_ref, pooled_ref, weight_ref, bias_ref, part_ref, back_ref, proj, target, grads
):
    y_n, h_n, x_n, l_n, c_n, two = dims
    near, per = x_n * l_n, c_n * two
    tokens, units = both_ref.shape[0], both_ref.shape[1] - LANES
    width = weight_ref.shape[1]
    half = width // c_n
    single = tokens // c_n
    core = core_ref[0]
    row = iota((tokens, tokens), 0)
    wanted = (
        (row // two) % c_n * single + row // single * (near * two) + row // per % near * two + row % two
    )
    turn = jnp.where(wanted == iota((tokens, tokens), 1), 1.0, 0.0).astype(BF)
    acts = both_ref[:, :units]
    step = 256
    s_pp = jnp.zeros((tokens, 1), F32)
    s_tt = jnp.zeros((tokens, 1), F32)
    s_pt = jnp.zeros((tokens, 1), F32)
    for at in range(0, width, step):
        cut = slice(at, at + step)
        p = jnp.dot(acts, weight_ref[:, cut], preferred_element_type=F32) + bias_ref[:, cut]
        t = jnp.dot(turn, pooled_ref[:, cut], preferred_element_type=F32)
        proj[:, cut] = p
        target[:, cut] = t
        s_pp = s_pp + jnp.sum(p * p, axis=1, keepdims=True)
        s_tt = s_tt + jnp.sum(t * t, axis=1, keepdims=True)
        s_pt = s_pt + jnp.sum(p * t, axis=1, keepdims=True)
    inv_proj = lax.rsqrt(s_pp + 1e-06)
    inv_target = lax.rsqrt(s_tt + 1e-06)
    cosine = s_pt * inv_proj * inv_target
    terms = both_ref[:, units:].astype(F32)
    cot = (terms[:, 2:3] + terms[:, 1:2]) + terms[:, 0:1]
    scale_t = inv_proj * inv_target
    scale_p = cosine * inv_proj * inv_proj
    y_blocks = width // y_n // LANES
    tail_row = iota((TAIL, step), 0)
    main = part_ref.shape[1] - TAIL
    for at in range(0, width, step):
        g = cot * (target[:, at : at + step] * scale_t - scale_p * proj[:, at : at + step])
        g = g.astype(BF)
        inside = at % half
        grads[at // half, :, inside : inside + step] = g
        total = jnp.sum(g.astype(F32), axis=0, keepdims=True)
        high = total.astype(BF).astype(F32)
        tail = jnp.where(tail_row == 0, high, jnp.where(tail_row == 1, total - high, 0.0)).astype(BF)
        for k in range(step // LANES):
            block = at // LANES + k
            piece = block // y_blocks * x_n + block % y_blocks
            part_ref[piece, main:, :] = tail[:, k * LANES : (k + 1) * LANES]
    for y in range(y_n):
        for x in range(y_blocks, x_n):
            part_ref[y * x_n + x, main:, :] = jnp.zeros((TAIL, LANES), BF)
    lane = iota((tokens, LANES), 1)
    high, low = split_two(cosine)
    spot = iota((tokens, LANES), 0) % per == lane
    owner = iota((near, tokens), 1) - core * single
    gather = jnp.where((owner >= 0) & (owner < single) & (owner // per == iota((near, tokens), 0)), 1.0, 0.0)
    gather = gather.astype(BF)
    back = jnp.zeros((near, LANES), F32)
    for term in (high, low):
        spread = jnp.where(spot, term.astype(F32), 0.0).astype(BF)
        back = back + jnp.dot(gather, spread, preferred_element_type=F32)
    back_ref[:near, :] = back
    back_ref[near:, :] = jnp.full((8, LANES), high_ref[0], I32).astype(F32)
    rows = units // y_n
    chunk = rows // h_n // x_n
    mine = grads[core]
    for y in range(y_n):
        product = lax.dot_general(
            acts[:, y * rows : (y + 1) * rows], mine, (((0,), (0,)), ((), ())), preferred_element_type=F32
        ).astype(BF)
        for h in range(h_n):
            for x in range(x_n):
                start = (h * x_n + x) * chunk
                for k in range(half // LANES):
                    to = (k * h_n + h) * chunk
                    part_ref[y * x_n + x, to : to + chunk, :] = product[
                        start : start + chunk, k * LANES : (k + 1) * LANES
                    ]


def plane_kernel(dims, part_ref, out_ref, spread):
    y_n, h_n, x_n, l_n, c_n, two = dims
    count, total_rows = part_ref.shape[0], part_ref.shape[1]
    main = total_rows - TAIL
    spread[...] = jnp.zeros_like(spread)
    group = out_ref.shape[0] // (h_n * l_n)
    lines = main // (h_n * l_n)

    def summed(start, size):
        total = part_ref[0, start : start + size, :].astype(F32)
        for p in range(1, count):
            total = total + part_ref[p, start : start + size, :].astype(F32)
        return total

    pair = lines // LINE_ROWS
    size = h_n * LINE_ROWS * l_n
    for k in range(pair):
        total = summed(k * size, size)
        for h in range(h_n):
            for r in range(LINE_ROWS):
                at = (h * LINE_ROWS + r) * l_n
                spread[pl.ds(h * l_n * group + k * LINE_ROWS + r, l_n, stride=group), :] = total[at : at + l_n]
    tail = summed(main, TAIL)
    bias = tail[0:1] + tail[1:2]
    high = bias.astype(BF).astype(F32)
    for r, value in enumerate((high, bias - high)):
        full = jnp.broadcast_to(value, (h_n * l_n, LANES))
        spread[pl.ds(lines + r, h_n * l_n, stride=group), :] = full
    out_ref[...] = spread[...].astype(BF)


def line_kernel(lines, part_ref, back_ref, out_ref):
    total = part_ref[0].astype(F32)
    for p in range(1, part_ref.shape[0]):
        total = total + part_ref[p].astype(F32)
    group = total.shape[0]
    row = iota((group, LANES), 0)
    bias = total[lines : lines + 1] + total[lines + 1 : lines + 2]
    high = bias.astype(BF).astype(F32)
    total = jnp.where(row == lines, high, jnp.where(row == lines + 1, bias - high, total))
    for p in range(out_ref.shape[0]):
        value = back_ref[p : p + 1, :]
        head = value.astype(BF).astype(F32)
        tile = jnp.where(row == group - 2, head, jnp.where(row == group - 1, value - head, total))
        out_ref[p] = tile.astype(BF)


def unpack_kernel(
    dims, back_ref, own_ref, both_ref, order_ref, cos_ref, weight_ref, bias_ref, wide, narrow
):
    y_n, h_n, x_n, l_n, c_n, two = dims
    near, per = x_n * l_n, c_n * two
    group = own_ref.shape[0] // near
    wide[...] = both_ref[...].astype(F32)
    narrow[...] = own_ref[...].astype(F32)
    half = weight_ref.shape[1] // c_n
    pairs = half // LANES
    lines = pairs * LINE_ROWS
    for c in range(c_n):
        for x in range(x_n):
            for k in range(pairs):
                for r in range(LINE_ROWS):
                    start = (c * near + x * l_n) * group + k * LINE_ROWS + r
                    to = (x * LINE_ROWS + r) * l_n
                    at = c * half + k * LANES
                    weight_ref[to : to + l_n, at : at + LANES] = wide[pl.ds(start, l_n, stride=group), :]
    cosines = narrow[pl.ds(group - 2, near, stride=group), :] + narrow[pl.ds(group - 1, near, stride=group), :]
    order = order_ref[...]
    tokens = order.shape[1]
    base = iota((near, tokens), 0) * per
    total = jnp.zeros((near, tokens), F32)
    for i in range(per):
        total = total + jnp.where(order == base + i, cosines[:, i : i + 1], 0.0)
    cos_ref[...] = jnp.sum(total, axis=0, keepdims=True)
    cols = bias_ref.shape[1]
    blocks = cols * h_n // LANES
    offset = back_ref[near:, :cols].astype(I32)[0:1] * cols
    out = jnp.zeros((8, cols), F32)
    for b in range(blocks):
        start = b * l_n * group + lines
        pick = iota((LANES, cols), 0) + b * LANES == iota((LANES, cols), 1) + offset
        pick = jnp.where(pick, 1.0, 0.0).astype(BF)
        for r in range(2):
            term = jnp.broadcast_to(narrow[start + r : start + r + 1, :], (8, LANES)).astype(BF)
            out = out + jnp.dot(term, pick, preferred_element_type=F32)
    bias_ref[...] = out[0:1]


def local(hidden, weight, bias, patches, slots, order, cotangent):
    y_n, h_n, x_n, l_n, c_n = (lax.axis_size(a) for a in ("y", "h", "x", "l", "c"))
    patches = patches[0]
    tokens, units = hidden.shape[1:]
    width = weight.shape[1]
    near = x_n * l_n
    per = tokens // near
    shards = near * c_n
    two = tokens // shards
    half = width // c_n
    dims = (y_n, h_n, x_n, l_n, c_n, two)
    shape = jax.ShapeDtypeStruct
    core = lax.axis_index("c").astype(I32)[None]
    high = lax.axis_index("h").astype(I32)[None]

    sent = call(send_kernel, shape((near, per, units + LANES), BF), [VMEM] * 3, limit=60)(
        hidden[0], order, cotangent
    )
    moved = lax.all_to_all(sent, ("x", "l"), 0, 0, tiled=True)
    pooled, weight = call(
        functools.partial(pool_kernel, dims),
        (shape((tokens, width), BF), shape(weight.shape, BF)),
        [VMEM, VMEM, pl.BlockSpec(memory_space=pl.ANY)],
        [pltpu.SemaphoreType.DMA],
    )(patches, slots, weight)
    pooled = lax.all_gather(pooled, "c", axis=0, tiled=True)

    both = lax.all_gather(moved.reshape(tokens, units + LANES), "c", axis=0, tiled=True)
    rows = units // (y_n * x_n)
    lines = half // LANES * LINE_ROWS
    part, back = call(
        functools.partial(middle_kernel, dims),
        (
            shape((y_n * x_n, rows * half // LANES + TAIL, LANES), BF),
            shape((near + 8, LANES), F32),
        ),
        [SMEM] * 2 + [VMEM] * 4,
        [
            pltpu.VMEM((c_n * tokens, width), F32),
            pltpu.VMEM((c_n * tokens, width), F32),
            pltpu.VMEM((c_n, c_n * tokens, half), BF),
        ],
    )(core, high, both, pooled, weight, bias[None, :])

    part = lax.all_to_all(part, ("y", "x"), 0, 0, tiled=True)
    spots = h_n * l_n
    part = call(
        functools.partial(plane_kernel, dims),
        shape((spots * TAIL, LANES), BF),
        [VMEM],
        [pltpu.VMEM((spots * TAIL, LANES), F32)],
    )(part)
    part, back = lax.optimization_barrier((part, back))
    part = lax.all_to_all(part.reshape(spots, TAIL, LANES), ("h", "l"), 0, 0, tiled=True)
    part = call(functools.partial(line_kernel, lines), shape((near, TAIL, LANES), BF), [VMEM] * 2)(part, back)
    part = lax.all_to_all(part, ("x", "l"), 0, 0, tiled=True).reshape(near * TAIL, LANES)
    wide = lax.all_gather(part, "c", axis=0, tiled=True)
    cos_sim, weight_grad, bias_grad = call(
        functools.partial(unpack_kernel, dims),
        (
            shape((1, tokens), F32),
            shape((units // (y_n * h_n), width), F32),
            shape((1, width // (y_n * h_n)), F32),
        ),
        [VMEM] * 4,
        [pltpu.VMEM((c_n * near * TAIL, LANES), F32), pltpu.VMEM((near * TAIL, LANES), F32)],
    )(back, part, wide, order)
    return cos_sim, weight_grad, bias_grad[0]


def solution(mesh, sizes=(4, 4, 4, 8, 2)):
    fine = Mesh(mesh.devices.reshape(sizes), ("y", "h", "x", "l", "c"))
    clip, seq = ("y", "h"), ("x", "l", "c")
    placed = (
        P(clip, seq, None),
        P(),
        P(),
        P(clip, seq, None),
        P(clip, seq),
        P(clip, seq),
        P(clip, seq),
    )
    return jax.shard_map(
        local,
        mesh=fine,
        in_specs=placed,
        out_specs=(P(clip, seq), P(clip, None), P(clip)),
        check_vma=False,
    )
```

```python
import functools

import jax
import jax.numpy as jnp
from jax import lax
from jax.experimental import pallas as pl
from jax.experimental.pallas import tpu as pltpu
from jax.sharding import Mesh, PartitionSpec as P

BF = jnp.bfloat16
F32 = jnp.float32
I32 = jnp.int32
LANES = 128
TAIL = 16
LINE_ROWS = 2
VMEM = pl.BlockSpec(memory_space=pltpu.VMEM)
SMEM = pl.BlockSpec(memory_space=pltpu.SMEM)


def iota(shape, axis):
    return lax.broadcasted_iota(I32, shape, axis)


def split_two(values):
    head = values.astype(BF)
    return head, (values - head.astype(F32)).astype(BF)


def call(body, outs, ins, scratch=(), limit=16):
    return pl.pallas_call(
        body,
        out_shape=outs,
        in_specs=ins,
        out_specs=jax.tree.map(lambda _: VMEM, outs),
        scratch_shapes=list(scratch),
        compiler_params=pltpu.CompilerParams(vmem_limit_bytes=limit << 20),
    )


def send_kernel(hidden_ref, order_ref, cot_ref, out_ref):
    tokens, units = hidden_ref.shape
    pieces, per = out_ref.shape[:2]
    pick = order_ref[...] == iota((tokens, tokens), 0)
    rows = jnp.dot(
        jnp.where(pick, 1.0, 0.0).astype(BF), hidden_ref[...], preferred_element_type=F32
    )
    cot = jnp.sum(jnp.where(pick, cot_ref[...], 0.0), axis=1, keepdims=True)
    high = cot.astype(BF).astype(F32)
    rest = cot - high
    middle = rest.astype(BF).astype(F32)
    low = rest - middle
    lane = iota((tokens, LANES), 1)
    cols = jnp.where(lane == 0, high, jnp.where(lane == 1, middle, jnp.where(lane == 2, low, 0.0)))
    for p in range(pieces):
        at = slice(p * per, (p + 1) * per)
        out_ref[p] = jnp.concatenate([rows[at], cols[at]], axis=1).astype(BF)


def pool_kernel(dims, patch_ref, slot_ref, pooled_ref):
    y_n, h_n, x_n, l_n, c_n, two = dims
    tokens, patches = pooled_ref.shape[0], patch_ref.shape[0]
    shape = (tokens, patches)
    row = iota(shape, 0)
    near = x_n * l_n
    src = row // two % near * c_n + row // (near * two)
    match = (iota(shape, 1) // (patches // (near * c_n)) == src) & (slot_ref[...] == row % two)
    match = jnp.where(match, 1.0, 0.0)
    counts = jnp.sum(match, axis=1, keepdims=True)
    totals = jnp.dot(match.astype(BF), patch_ref[...], preferred_element_type=F32)
    pooled_ref[...] = (totals / counts).astype(BF)


def middle_kernel(
    dims, core_ref, high_ref, both_ref, pooled_ref, other_ref, weight_ref, bias_ref, part_ref, back_ref, proj, target, grads
):
    y_n, h_n, x_n, l_n, c_n, two = dims
    near, per = x_n * l_n, c_n * two
    tokens, units = both_ref.shape[0], both_ref.shape[1] - LANES
    width = weight_ref.shape[1]
    half = width // c_n
    single = tokens // c_n
    core = core_ref[0]
    row = iota((tokens, single), 0)
    wanted = row // single * (near * two) + row // per % near * two + row % two
    place = wanted == iota((tokens, single), 1)
    ours = row // two % c_n == core
    turn = jnp.where(place & ours, 1.0, 0.0).astype(BF)
    turn_other = jnp.where(place & (row // two % c_n != core), 1.0, 0.0).astype(BF)
    acts = both_ref[:, :units]
    step = 256
    s_pp = jnp.zeros((tokens, 1), F32)
    s_tt = jnp.zeros((tokens, 1), F32)
    s_pt = jnp.zeros((tokens, 1), F32)
    for at in range(0, width, step):
        cut = slice(at, at + step)
        p = jnp.dot(acts, weight_ref[:, cut], preferred_element_type=F32) + bias_ref[:, cut]
        t = jnp.dot(turn, pooled_ref[:, cut], preferred_element_type=F32)
        t = t + jnp.dot(turn_other, other_ref[:, cut], preferred_element_type=F32)
        proj[:, cut] = p
        target[:, cut] = t
        s_pp = s_pp + jnp.sum(p * p, axis=1, keepdims=True)
        s_tt = s_tt + jnp.sum(t * t, axis=1, keepdims=True)
        s_pt = s_pt + jnp.sum(p * t, axis=1, keepdims=True)
    inv_proj = lax.rsqrt(s_pp + 1e-06)
    inv_target = lax.rsqrt(s_tt + 1e-06)
    cosine = s_pt * inv_proj * inv_target
    terms = both_ref[:, units:].astype(F32)
    cot = (terms[:, 2:3] + terms[:, 1:2]) + terms[:, 0:1]
    scale_t = inv_proj * inv_target
    scale_p = cosine * inv_proj * inv_proj
    y_blocks = width // y_n // LANES
    tail_row = iota((TAIL, step), 0)
    main = part_ref.shape[1] - TAIL
    for at in range(0, width, step):
        g = cot * (target[:, at : at + step] * scale_t - scale_p * proj[:, at : at + step])
        g = g.astype(BF)
        inside = at % half
        grads[at // half, :, inside : inside + step] = g
        total = jnp.sum(g.astype(F32), axis=0, keepdims=True)
        high = total.astype(BF).astype(F32)
        tail = jnp.where(tail_row == 0, high, jnp.where(tail_row == 1, total - high, 0.0)).astype(BF)
        for k in range(step // LANES):
            block = at // LANES + k
            piece = block // y_blocks * x_n + block % y_blocks
            part_ref[piece, main:, :] = tail[:, k * LANES : (k + 1) * LANES]
    for y in range(y_n):
        for x in range(y_blocks, x_n):
            part_ref[y * x_n + x, main:, :] = jnp.zeros((TAIL, LANES), BF)
    lane = iota((tokens, LANES), 1)
    high, low = split_two(cosine)
    spot = iota((tokens, LANES), 0) % per == lane
    owner = iota((near, tokens), 1) - core * single
    gather = jnp.where((owner >= 0) & (owner < single) & (owner // per == iota((near, tokens), 0)), 1.0, 0.0)
    gather = gather.astype(BF)
    back = jnp.zeros((near, LANES), F32)
    for term in (high, low):
        spread = jnp.where(spot, term.astype(F32), 0.0).astype(BF)
        back = back + jnp.dot(gather, spread, preferred_element_type=F32)
    back_ref[:near, :] = back
    back_ref[near:, :] = jnp.full((8, LANES), high_ref[0], I32).astype(F32)
    rows = units // y_n
    chunk = rows // h_n // x_n
    mine = grads[core]
    for y in range(y_n):
        product = lax.dot_general(
            acts[:, y * rows : (y + 1) * rows], mine, (((0,), (0,)), ((), ())), preferred_element_type=F32
        ).astype(BF)
        for h in range(h_n):
            for x in range(x_n):
                start = (h * x_n + x) * chunk
                for k in range(half // LANES):
                    to = (k * h_n + h) * chunk
                    part_ref[y * x_n + x, to : to + chunk, :] = product[
                        start : start + chunk, k * LANES : (k + 1) * LANES
                    ]


def plane_kernel(dims, part_ref, out_ref, spread):
    y_n, h_n, x_n, l_n, c_n, two = dims
    count, total_rows = part_ref.shape[0], part_ref.shape[1]
    main = total_rows - TAIL
    spread[...] = jnp.zeros_like(spread)
    group = out_ref.shape[0] // (h_n * l_n)
    lines = main // (h_n * l_n)

    def summed(start, size):
        total = part_ref[0, start : start + size, :].astype(F32)
        for p in range(1, count):
            total = total + part_ref[p, start : start + size, :].astype(F32)
        return total

    pair = lines // LINE_ROWS
    size = h_n * LINE_ROWS * l_n
    for k in range(pair):
        total = summed(k * size, size)
        for h in range(h_n):
            for r in range(LINE_ROWS):
                at = (h * LINE_ROWS + r) * l_n
                spread[pl.ds(h * l_n * group + k * LINE_ROWS + r, l_n, stride=group), :] = total[at : at + l_n]
    tail = summed(main, TAIL)
    bias = tail[0:1] + tail[1:2]
    high = bias.astype(BF).astype(F32)
    for r, value in enumerate((high, bias - high)):
        full = jnp.broadcast_to(value, (h_n * l_n, LANES))
        spread[pl.ds(lines + r, h_n * l_n, stride=group), :] = full
    out_ref[...] = spread[...].astype(BF)


def line_kernel(lines, part_ref, back_ref, out_ref):
    total = part_ref[0].astype(F32)
    for p in range(1, part_ref.shape[0]):
        total = total + part_ref[p].astype(F32)
    group = total.shape[0]
    row = iota((group, LANES), 0)
    bias = total[lines : lines + 1] + total[lines + 1 : lines + 2]
    high = bias.astype(BF).astype(F32)
    total = jnp.where(row == lines, high, jnp.where(row == lines + 1, bias - high, total))
    for p in range(out_ref.shape[0]):
        value = back_ref[p : p + 1, :]
        head = value.astype(BF).astype(F32)
        tile = jnp.where(row == group - 2, head, jnp.where(row == group - 1, value - head, total))
        out_ref[p] = tile.astype(BF)


def unpack_kernel(
    dims, back_ref, own_ref, both_ref, order_ref, cos_ref, weight_ref, bias_ref, wide, narrow
):
    y_n, h_n, x_n, l_n, c_n, two = dims
    near, per = x_n * l_n, c_n * two
    group = own_ref.shape[0] // near
    wide[...] = both_ref[...].astype(F32)
    narrow[...] = own_ref[...].astype(F32)
    half = weight_ref.shape[1] // c_n
    pairs = half // LANES
    lines = pairs * LINE_ROWS
    for c in range(c_n):
        for x in range(x_n):
            for k in range(pairs):
                for r in range(LINE_ROWS):
                    start = (c * near + x * l_n) * group + k * LINE_ROWS + r
                    to = (x * LINE_ROWS + r) * l_n
                    at = c * half + k * LANES
                    weight_ref[to : to + l_n, at : at + LANES] = wide[pl.ds(start, l_n, stride=group), :]
    cosines = narrow[pl.ds(group - 2, near, stride=group), :] + narrow[pl.ds(group - 1, near, stride=group), :]
    order = order_ref[...]
    tokens = order.shape[1]
    base = iota((near, tokens), 0) * per
    total = jnp.zeros((near, tokens), F32)
    for i in range(per):
        total = total + jnp.where(order == base + i, cosines[:, i : i + 1], 0.0)
    cos_ref[...] = jnp.sum(total, axis=0, keepdims=True)
    cols = bias_ref.shape[1]
    blocks = cols * h_n // LANES
    offset = back_ref[near:, :cols].astype(I32)[0:1] * cols
    out = jnp.zeros((8, cols), F32)
    for b in range(blocks):
        start = b * l_n * group + lines
        pick = iota((LANES, cols), 0) + b * LANES == iota((LANES, cols), 1) + offset
        pick = jnp.where(pick, 1.0, 0.0).astype(BF)
        for r in range(2):
            term = jnp.broadcast_to(narrow[start + r : start + r + 1, :], (8, LANES)).astype(BF)
            out = out + jnp.dot(term, pick, preferred_element_type=F32)
    bias_ref[...] = out[0:1]


def local(hidden, weight, bias, patches, slots, order, cotangent):
    y_n, h_n, x_n, l_n, c_n = (lax.axis_size(a) for a in ("y", "h", "x", "l", "c"))
    patches = patches[0]
    tokens, units = hidden.shape[1:]
    width = weight.shape[1]
    near = x_n * l_n
    per = tokens // near
    shards = near * c_n
    two = tokens // shards
    half = width // c_n
    dims = (y_n, h_n, x_n, l_n, c_n, two)
    shape = jax.ShapeDtypeStruct
    core = lax.axis_index("c").astype(I32)[None]
    high = lax.axis_index("h").astype(I32)[None]

    sent = call(send_kernel, shape((near, per, units + LANES), BF), [VMEM] * 3, limit=60)(
        hidden[0], order, cotangent
    )
    moved = lax.all_to_all(sent, ("x", "l"), 0, 0, tiled=True)
    pooled = call(
        functools.partial(pool_kernel, dims), shape((tokens, width), BF), [VMEM] * 2, limit=8
    )(patches, slots)
    other = lax.ppermute(pooled, "c", [(c, (c + 1) % c_n) for c in range(c_n)])

    both = lax.all_gather(moved.reshape(tokens, units + LANES), "c", axis=0, tiled=True)
    rows = units // (y_n * x_n)
    lines = half // LANES * LINE_ROWS
    part, back = call(
        functools.partial(middle_kernel, dims),
        (
            shape((y_n * x_n, rows * half // LANES + TAIL, LANES), BF),
            shape((near + 8, LANES), F32),
        ),
        [SMEM] * 2 + [VMEM] * 5,
        [
            pltpu.VMEM((c_n * tokens, width), F32),
            pltpu.VMEM((c_n * tokens, width), F32),
            pltpu.VMEM((c_n, c_n * tokens, half), BF),
        ],
    )(core, high, both, pooled, other, weight, bias[None, :])

    part = lax.all_to_all(part, ("y", "x"), 0, 0, tiled=True)
    spots = h_n * l_n
    part = call(
        functools.partial(plane_kernel, dims),
        shape((spots * TAIL, LANES), BF),
        [VMEM],
        [pltpu.VMEM((spots * TAIL, LANES), F32)],
    )(part)
    part, back = lax.optimization_barrier((part, back))
    part = lax.all_to_all(part.reshape(spots, TAIL, LANES), ("h", "l"), 0, 0, tiled=True)
    part = call(functools.partial(line_kernel, lines), shape((near, TAIL, LANES), BF), [VMEM] * 2)(part, back)
    part = lax.all_to_all(part, ("x", "l"), 0, 0, tiled=True).reshape(near * TAIL, LANES)
    wide = lax.all_gather(part, "c", axis=0, tiled=True)
    cos_sim, weight_grad, bias_grad = call(
        functools.partial(unpack_kernel, dims),
        (
            shape((1, tokens), F32),
            shape((units // (y_n * h_n), width), F32),
            shape((1, width // (y_n * h_n)), F32),
        ),
        [VMEM] * 4,
        [pltpu.VMEM((c_n * near * TAIL, LANES), F32), pltpu.VMEM((near * TAIL, LANES), F32)],
    )(back, part, wide, order)
    return cos_sim, weight_grad, bias_grad[0]


def solution(mesh, sizes=(4, 4, 4, 8, 2)):
    fine = Mesh(mesh.devices.reshape(sizes), ("y", "h", "x", "l", "c"))
    clip, seq = ("y", "h"), ("x", "l", "c")
    placed = (
        P(clip, seq, None),
        P(),
        P(),
        P(clip, seq, None),
        P(clip, seq),
        P(clip, seq),
        P(clip, seq),
    )
    return jax.shard_map(
        local,
        mesh=fine,
        in_specs=placed,
        out_specs=(P(clip, seq), P(clip, None), P(clip)),
        check_vma=False,
    )
```

```python
import functools

import jax
import jax.numpy as jnp
from jax import lax
from jax.experimental import pallas as pl
from jax.experimental.pallas import tpu as pltpu
from jax.sharding import Mesh, PartitionSpec as P

BF = jnp.bfloat16
F32 = jnp.float32
I32 = jnp.int32
LANES = 128
TAIL = 16
LINE_ROWS = 2
VMEM = pl.BlockSpec(memory_space=pltpu.VMEM)
SMEM = pl.BlockSpec(memory_space=pltpu.SMEM)


def iota(shape, axis):
    return lax.broadcasted_iota(I32, shape, axis)


def split_two(values):
    head = values.astype(BF)
    return head, (values - head.astype(F32)).astype(BF)


def call(body, outs, ins, scratch=(), limit=16):
    return pl.pallas_call(
        body,
        out_shape=outs,
        in_specs=ins,
        out_specs=jax.tree.map(lambda _: VMEM, outs),
        scratch_shapes=list(scratch),
        compiler_params=pltpu.CompilerParams(vmem_limit_bytes=limit << 20),
    )


def send_kernel(hidden_ref, order_ref, cot_ref, out_ref):
    tokens, units = hidden_ref.shape
    pieces, per = out_ref.shape[:2]
    pick = order_ref[...] == iota((tokens, tokens), 0)
    rows = jnp.dot(
        jnp.where(pick, 1.0, 0.0).astype(BF), hidden_ref[...], preferred_element_type=F32
    )
    cot = jnp.sum(jnp.where(pick, cot_ref[...], 0.0), axis=1, keepdims=True)
    high = cot.astype(BF).astype(F32)
    rest = cot - high
    middle = rest.astype(BF).astype(F32)
    low = rest - middle
    lane = iota((tokens, LANES), 1)
    cols = jnp.where(lane == 0, high, jnp.where(lane == 1, middle, jnp.where(lane == 2, low, 0.0)))
    for p in range(pieces):
        at = slice(p * per, (p + 1) * per)
        out_ref[p] = jnp.concatenate([rows[at], cols[at]], axis=1).astype(BF)


def middle_kernel(
    dims, core_ref, high_ref, both_ref, pooled_ref, weight_ref, bias_ref, part_ref, back_ref,
    proj, target, grads, held, sems
):
    y_n, h_n, x_n, l_n, c_n, two = dims
    near, per = x_n * l_n, c_n * two
    tokens, units = both_ref.shape[0], both_ref.shape[1] - LANES
    width = weight_ref.shape[1]
    half = width // c_n
    single = tokens // c_n
    core = core_ref[0]
    fetch = []
    for k in range(sems.shape[0]):
        cut = pl.ds(k * (width // sems.shape[0]), width // sems.shape[0])
        fetch.append(pltpu.make_async_copy(weight_ref.at[:, cut], held.at[:, cut], sems.at[k]))
        fetch[-1].start()
    row = iota((tokens, tokens), 0)
    wanted = (
        (row // two) % c_n * single + row // single * (near * two) + row // per % near * two + row % two
    )
    turn = jnp.where(wanted == iota((tokens, tokens), 1), 1.0, 0.0).astype(BF)
    acts = both_ref[:, :units]
    step = 256
    s_pp = jnp.zeros((tokens, 1), F32)
    s_tt = jnp.zeros((tokens, 1), F32)
    s_pt = jnp.zeros((tokens, 1), F32)
    for at in range(0, width, step):
        cut = slice(at, at + step)
        t = jnp.dot(turn, pooled_ref[:, cut], preferred_element_type=F32)
        target[:, cut] = t
        s_tt = s_tt + jnp.sum(t * t, axis=1, keepdims=True)
    for at in range(0, width, step):
        cut = slice(at, at + step)
        fetch[at // step].wait()
        p = jnp.dot(acts, held[:, cut], preferred_element_type=F32) + bias_ref[:, cut]
        proj[:, cut] = p
        s_pp = s_pp + jnp.sum(p * p, axis=1, keepdims=True)
        s_pt = s_pt + jnp.sum(p * target[:, cut], axis=1, keepdims=True)
    inv_proj = lax.rsqrt(s_pp + 1e-06)
    inv_target = lax.rsqrt(s_tt + 1e-06)
    cosine = s_pt * inv_proj * inv_target
    terms = both_ref[:, units:].astype(F32)
    cot = (terms[:, 2:3] + terms[:, 1:2]) + terms[:, 0:1]
    scale_t = inv_proj * inv_target
    scale_p = cosine * inv_proj * inv_proj
    y_blocks = width // y_n // LANES
    tail_row = iota((TAIL, step), 0)
    main = part_ref.shape[1] - TAIL
    for at in range(0, width, step):
        g = cot * (target[:, at : at + step] * scale_t - scale_p * proj[:, at : at + step])
        g = g.astype(BF)
        inside = at % half
        grads[at // half, :, inside : inside + step] = g
        total = jnp.sum(g.astype(F32), axis=0, keepdims=True)
        high = total.astype(BF).astype(F32)
        tail = jnp.where(tail_row == 0, high, jnp.where(tail_row == 1, total - high, 0.0)).astype(BF)
        for k in range(step // LANES):
            block = at // LANES + k
            piece = block // y_blocks * x_n + block % y_blocks
            part_ref[piece, main:, :] = tail[:, k * LANES : (k + 1) * LANES]
    for y in range(y_n):
        for x in range(y_blocks, x_n):
            part_ref[y * x_n + x, main:, :] = jnp.zeros((TAIL, LANES), BF)
    lane = iota((tokens, LANES), 1)
    high, low = split_two(cosine)
    spot = iota((tokens, LANES), 0) % per == lane
    owner = iota((near, tokens), 1) - core * single
    gather = jnp.where((owner >= 0) & (owner < single) & (owner // per == iota((near, tokens), 0)), 1.0, 0.0)
    gather = gather.astype(BF)
    back = jnp.zeros((near, LANES), F32)
    for term in (high, low):
        spread = jnp.where(spot, term.astype(F32), 0.0).astype(BF)
        back = back + jnp.dot(gather, spread, preferred_element_type=F32)
    back_ref[:near, :] = back
    back_ref[near:, :] = jnp.full((8, LANES), high_ref[0], I32).astype(F32)
    rows = units // y_n
    chunk = rows // h_n // x_n
    mine = grads[core]
    for y in range(y_n):
        product = lax.dot_general(
            acts[:, y * rows : (y + 1) * rows], mine, (((0,), (0,)), ((), ())), preferred_element_type=F32
        ).astype(BF)
        for h in range(h_n):
            for x in range(x_n):
                start = (h * x_n + x) * chunk
                for k in range(half // LANES):
                    to = (k * h_n + h) * chunk
                    part_ref[y * x_n + x, to : to + chunk, :] = product[
                        start : start + chunk, k * LANES : (k + 1) * LANES
                    ]


def plane_kernel(dims, part_ref, out_ref, spread):
    y_n, h_n, x_n, l_n, c_n, two = dims
    count, total_rows = part_ref.shape[0], part_ref.shape[1]
    main = total_rows - TAIL
    spread[...] = jnp.zeros_like(spread)
    group = out_ref.shape[0] // (h_n * l_n)
    lines = main // (h_n * l_n)

    def summed(start, size):
        total = part_ref[0, start : start + size, :].astype(F32)
        for p in range(1, count):
            total = total + part_ref[p, start : start + size, :].astype(F32)
        return total

    pair = lines // LINE_ROWS
    size = h_n * LINE_ROWS * l_n
    for k in range(pair):
        total = summed(k * size, size)
        for h in range(h_n):
            for r in range(LINE_ROWS):
                at = (h * LINE_ROWS + r) * l_n
                spread[pl.ds(h * l_n * group + k * LINE_ROWS + r, l_n, stride=group), :] = total[at : at + l_n]
    tail = summed(main, TAIL)
    bias = tail[0:1] + tail[1:2]
    high = bias.astype(BF).astype(F32)
    for r, value in enumerate((high, bias - high)):
        full = jnp.broadcast_to(value, (h_n * l_n, LANES))
        spread[pl.ds(lines + r, h_n * l_n, stride=group), :] = full
    out_ref[...] = spread[...].astype(BF)


def line_kernel(lines, part_ref, back_ref, out_ref):
    total = part_ref[0].astype(F32)
    for p in range(1, part_ref.shape[0]):
        total = total + part_ref[p].astype(F32)
    group = total.shape[0]
    row = iota((group, LANES), 0)
    bias = total[lines : lines + 1] + total[lines + 1 : lines + 2]
    high = bias.astype(BF).astype(F32)
    total = jnp.where(row == lines, high, jnp.where(row == lines + 1, bias - high, total))
    for p in range(out_ref.shape[0]):
        value = back_ref[p : p + 1, :]
        head = value.astype(BF).astype(F32)
        tile = jnp.where(row == group - 2, head, jnp.where(row == group - 1, value - head, total))
        out_ref[p] = tile.astype(BF)


def unpack_kernel(
    dims, back_ref, own_ref, both_ref, order_ref, cos_ref, weight_ref, bias_ref, wide, narrow
):
    y_n, h_n, x_n, l_n, c_n, two = dims
    near, per = x_n * l_n, c_n * two
    group = own_ref.shape[0] // near
    wide[...] = both_ref[...].astype(F32)
    narrow[...] = own_ref[...].astype(F32)
    half = weight_ref.shape[1] // c_n
    pairs = half // LANES
    lines = pairs * LINE_ROWS
    for c in range(c_n):
        for x in range(x_n):
            for k in range(pairs):
                for r in range(LINE_ROWS):
                    start = (c * near + x * l_n) * group + k * LINE_ROWS + r
                    to = (x * LINE_ROWS + r) * l_n
                    at = c * half + k * LANES
                    weight_ref[to : to + l_n, at : at + LANES] = wide[pl.ds(start, l_n, stride=group), :]
    cosines = narrow[pl.ds(group - 2, near, stride=group), :] + narrow[pl.ds(group - 1, near, stride=group), :]
    order = order_ref[...]
    tokens = order.shape[1]
    base = iota((near, tokens), 0) * per
    total = jnp.zeros((near, tokens), F32)
    for i in range(per):
        total = total + jnp.where(order == base + i, cosines[:, i : i + 1], 0.0)
    cos_ref[...] = jnp.sum(total, axis=0, keepdims=True)
    cols = bias_ref.shape[1]
    blocks = cols * h_n // LANES
    offset = back_ref[near:, :cols].astype(I32)[0:1] * cols
    out = jnp.zeros((8, cols), F32)
    for b in range(blocks):
        start = b * l_n * group + lines
        pick = iota((LANES, cols), 0) + b * LANES == iota((LANES, cols), 1) + offset
        pick = jnp.where(pick, 1.0, 0.0).astype(BF)
        for r in range(2):
            term = jnp.broadcast_to(narrow[start + r : start + r + 1, :], (8, LANES)).astype(BF)
            out = out + jnp.dot(term, pick, preferred_element_type=F32)
    bias_ref[...] = out[0:1]


def local(hidden, weight, bias, patches, slots, order, cotangent):
    y_n, h_n, x_n, l_n, c_n = (lax.axis_size(a) for a in ("y", "h", "x", "l", "c"))
    patches = patches[0]
    tokens, units = hidden.shape[1:]
    width = weight.shape[1]
    near = x_n * l_n
    per = tokens // near
    shards = near * c_n
    two = tokens // shards
    half = width // c_n
    dims = (y_n, h_n, x_n, l_n, c_n, two)
    shape = jax.ShapeDtypeStruct
    core = lax.axis_index("c").astype(I32)[None]
    high = lax.axis_index("h").astype(I32)[None]

    sent = call(send_kernel, shape((near, per, units + LANES), BF), [VMEM] * 3, limit=60)(
        hidden[0], order, cotangent
    )
    moved = lax.all_to_all(sent, ("x", "l"), 0, 0, tiled=True)
    at = jnp.arange(tokens, dtype=I32)
    src = (at // two) % near * c_n + at // (near * two)
    block = patches.shape[0] // (near * c_n)
    q = jnp.arange(patches.shape[0], dtype=I32)
    match = (q[None, :] // block == src[:, None]) & (slots[0][None, :] == (at % two)[:, None])
    totals = jnp.dot(match.astype(BF), patches, preferred_element_type=F32)
    pooled = (totals / jnp.sum(match.astype(F32), axis=1)[:, None]).astype(BF)
    pooled = lax.all_gather(pooled, "c", axis=0, tiled=True)

    both = lax.all_gather(moved.reshape(tokens, units + LANES), "c", axis=0, tiled=True)
    rows = units // (y_n * x_n)
    lines = half // LANES * LINE_ROWS
    part, back = call(
        functools.partial(middle_kernel, dims),
        (
            shape((y_n * x_n, rows * half // LANES + TAIL, LANES), BF),
            shape((near + 8, LANES), F32),
        ),
        [SMEM] * 2 + [VMEM] * 2 + [pl.BlockSpec(memory_space=pl.ANY), VMEM],
        [
            pltpu.VMEM((c_n * tokens, width), F32),
            pltpu.VMEM((c_n * tokens, width), F32),
            pltpu.VMEM((c_n, c_n * tokens, half), BF),
            pltpu.VMEM((units, width), BF),
            pltpu.SemaphoreType.DMA((width // 256,)),
        ],
        limit=50,
    )(core, high, both, pooled, weight, bias[None, :])

    part = lax.all_to_all(part, ("y", "x"), 0, 0, tiled=True)
    spots = h_n * l_n
    part = call(
        functools.partial(plane_kernel, dims),
        shape((spots * TAIL, LANES), BF),
        [VMEM],
        [pltpu.VMEM((spots * TAIL, LANES), F32)],
    )(part)
    part, back = lax.optimization_barrier((part, back))
    part = lax.all_to_all(part.reshape(spots, TAIL, LANES), ("h", "l"), 0, 0, tiled=True)
    part = call(functools.partial(line_kernel, lines), shape((near, TAIL, LANES), BF), [VMEM] * 2)(part, back)
    part = lax.all_to_all(part, ("x", "l"), 0, 0, tiled=True).reshape(near * TAIL, LANES)
    wide = lax.all_gather(part, "c", axis=0, tiled=True)
    cos_sim, weight_grad, bias_grad = call(
        functools.partial(unpack_kernel, dims),
        (
            shape((1, tokens), F32),
            shape((units // (y_n * h_n), width), F32),
            shape((1, width // (y_n * h_n)), F32),
        ),
        [VMEM] * 4,
        [pltpu.VMEM((c_n * near * TAIL, LANES), F32), pltpu.VMEM((near * TAIL, LANES), F32)],
    )(back, part, wide, order)
    return cos_sim, weight_grad, bias_grad[0]


def solution(mesh, sizes=(4, 4, 4, 8, 2)):
    fine = Mesh(mesh.devices.reshape(sizes), ("y", "h", "x", "l", "c"))
    clip, seq = ("y", "h"), ("x", "l", "c")
    placed = (
        P(clip, seq, None),
        P(),
        P(),
        P(clip, seq, None),
        P(clip, seq),
        P(clip, seq),
        P(clip, seq),
    )
    return jax.shard_map(
        local,
        mesh=fine,
        in_specs=placed,
        out_specs=(P(clip, seq), P(clip, None), P(clip)),
        check_vma=False,
    )
```

```python
import functools

import jax
import jax.numpy as jnp
from jax import lax
from jax.experimental import pallas as pl
from jax.experimental.pallas import tpu as pltpu
from jax.sharding import Mesh, PartitionSpec as P

BF = jnp.bfloat16
F32 = jnp.float32
I32 = jnp.int32
LANES = 128
TAIL = 16
LINE_ROWS = 2
VMEM = pl.BlockSpec(memory_space=pltpu.VMEM)
SMEM = pl.BlockSpec(memory_space=pltpu.SMEM)


def iota(shape, axis):
    return lax.broadcasted_iota(I32, shape, axis)


def split_two(values):
    head = values.astype(BF)
    return head, (values - head.astype(F32)).astype(BF)


def call(body, outs, ins, scratch=(), limit=16):
    return pl.pallas_call(
        body,
        out_shape=outs,
        in_specs=ins,
        out_specs=jax.tree.map(lambda _: VMEM, outs),
        scratch_shapes=list(scratch),
        compiler_params=pltpu.CompilerParams(vmem_limit_bytes=limit << 20),
    )


def send_kernel(hidden_ref, order_ref, cot_ref, out_ref):
    tokens, units = hidden_ref.shape
    pieces, per = out_ref.shape[:2]
    pick = order_ref[...] == iota((tokens, tokens), 0)
    rows = jnp.dot(
        jnp.where(pick, 1.0, 0.0).astype(BF), hidden_ref[...], preferred_element_type=F32
    )
    cot = jnp.sum(jnp.where(pick, cot_ref[...], 0.0), axis=1, keepdims=True)
    high = cot.astype(BF).astype(F32)
    rest = cot - high
    middle = rest.astype(BF).astype(F32)
    low = rest - middle
    lane = iota((tokens, LANES), 1)
    cols = jnp.where(lane == 0, high, jnp.where(lane == 1, middle, jnp.where(lane == 2, low, 0.0)))
    for p in range(pieces):
        at = slice(p * per, (p + 1) * per)
        out_ref[p] = jnp.concatenate([rows[at], cols[at]], axis=1).astype(BF)


def pool_kernel(dims, patch_ref, slot_ref, pooled_ref):
    y_n, h_n, x_n, l_n, c_n, two = dims
    tokens, patches = pooled_ref.shape[0], patch_ref.shape[0]
    shape = (tokens, patches)
    row = iota(shape, 0)
    near = x_n * l_n
    src = row // two % near * c_n + row // (near * two)
    match = (iota(shape, 1) // (patches // (near * c_n)) == src) & (slot_ref[...] == row % two)
    match = jnp.where(match, 1.0, 0.0)
    counts = jnp.sum(match, axis=1, keepdims=True)
    totals = jnp.dot(match.astype(BF), patch_ref[...], preferred_element_type=F32)
    pooled_ref[...] = (totals / counts).astype(BF)


def middle_kernel(
    dims, core_ref, high_ref, both_ref, pooled_ref, weight_ref, bias_ref, part_ref, back_ref,
    proj, target, grads, rows_held, acts, pooled, sem
):
    y_n, h_n, x_n, l_n, c_n, two = dims
    near, per = x_n * l_n, c_n * two
    tokens, units = acts.shape
    fetch = pltpu.make_async_copy(pooled_ref, pooled, sem)
    fetch.start()
    for p in range(both_ref.shape[0]):
        rows_held[p * per : (p + 1) * per, :] = both_ref[p].astype(F32)
    acts[...] = rows_held[:, :units].astype(BF)
    width = weight_ref.shape[1]
    half = width // c_n
    single = tokens // c_n
    core = core_ref[0]
    row = iota((tokens, tokens), 0)
    wanted = (
        (row // two) % c_n * single + row // single * (near * two) + row // per % near * two + row % two
    )
    turn = jnp.where(wanted == iota((tokens, tokens), 1), 1.0, 0.0).astype(BF)
    step = 256
    s_pp = jnp.zeros((tokens, 1), F32)
    s_tt = jnp.zeros((tokens, 1), F32)
    s_pt = jnp.zeros((tokens, 1), F32)
    for at in range(0, width, step):
        cut = slice(at, at + step)
        p = jnp.dot(acts[...], weight_ref[:, cut], preferred_element_type=F32) + bias_ref[:, cut]
        proj[:, cut] = p
        s_pp = s_pp + jnp.sum(p * p, axis=1, keepdims=True)
    fetch.wait()
    for at in range(0, width, step):
        cut = slice(at, at + step)
        t = jnp.dot(turn, pooled[:, cut], preferred_element_type=F32)
        target[:, cut] = t
        s_tt = s_tt + jnp.sum(t * t, axis=1, keepdims=True)
        s_pt = s_pt + jnp.sum(proj[:, cut] * t, axis=1, keepdims=True)
    inv_proj = lax.rsqrt(s_pp + 1e-06)
    inv_target = lax.rsqrt(s_tt + 1e-06)
    cosine = s_pt * inv_proj * inv_target
    terms = rows_held[:, units:]
    cot = (terms[:, 2:3] + terms[:, 1:2]) + terms[:, 0:1]
    scale_t = inv_proj * inv_target
    scale_p = cosine * inv_proj * inv_proj
    y_blocks = width // y_n // LANES
    tail_row = iota((TAIL, step), 0)
    main = part_ref.shape[1] - TAIL
    for at in range(0, width, step):
        g = cot * (target[:, at : at + step] * scale_t - scale_p * proj[:, at : at + step])
        g = g.astype(BF)
        inside = at % half
        grads[at // half, :, inside : inside + step] = g
        total = jnp.sum(g.astype(F32), axis=0, keepdims=True)
        high = total.astype(BF).astype(F32)
        tail = jnp.where(tail_row == 0, high, jnp.where(tail_row == 1, total - high, 0.0)).astype(BF)
        for k in range(step // LANES):
            block = at // LANES + k
            piece = block // y_blocks * x_n + block % y_blocks
            part_ref[piece, main:, :] = tail[:, k * LANES : (k + 1) * LANES]
    for y in range(y_n):
        for x in range(y_blocks, x_n):
            part_ref[y * x_n + x, main:, :] = jnp.zeros((TAIL, LANES), BF)
    lane = iota((tokens, LANES), 1)
    high, low = split_two(cosine)
    spot = iota((tokens, LANES), 0) % per == lane
    owner = iota((near, tokens), 1) - core * single
    gather = jnp.where((owner >= 0) & (owner < single) & (owner // per == iota((near, tokens), 0)), 1.0, 0.0)
    gather = gather.astype(BF)
    back = jnp.zeros((near, LANES), F32)
    for term in (high, low):
        spread = jnp.where(spot, term.astype(F32), 0.0).astype(BF)
        back = back + jnp.dot(gather, spread, preferred_element_type=F32)
    back_ref[:near, :] = back
    back_ref[near:, :] = jnp.full((8, LANES), high_ref[0], I32).astype(F32)
    rows = units // y_n
    chunk = rows // h_n // x_n
    mine = grads[core]
    for y in range(y_n):
        product = lax.dot_general(
            acts[:, y * rows : (y + 1) * rows], mine, (((0,), (0,)), ((), ())), preferred_element_type=F32
        ).astype(BF)
        for h in range(h_n):
            for x in range(x_n):
                start = (h * x_n + x) * chunk
                for k in range(half // LANES):
                    to = (k * h_n + h) * chunk
                    part_ref[y * x_n + x, to : to + chunk, :] = product[
                        start : start + chunk, k * LANES : (k + 1) * LANES
                    ]


def plane_kernel(dims, part_ref, out_ref, spread):
    y_n, h_n, x_n, l_n, c_n, two = dims
    count, total_rows = part_ref.shape[0], part_ref.shape[1]
    main = total_rows - TAIL
    spread[...] = jnp.zeros_like(spread)
    group = out_ref.shape[0] // (h_n * l_n)
    lines = main // (h_n * l_n)

    def summed(start, size):
        total = part_ref[0, start : start + size, :].astype(F32)
        for p in range(1, count):
            total = total + part_ref[p, start : start + size, :].astype(F32)
        return total

    pair = lines // LINE_ROWS
    size = h_n * LINE_ROWS * l_n
    for k in range(pair):
        total = summed(k * size, size)
        for h in range(h_n):
            for r in range(LINE_ROWS):
                at = (h * LINE_ROWS + r) * l_n
                spread[pl.ds(h * l_n * group + k * LINE_ROWS + r, l_n, stride=group), :] = total[at : at + l_n]
    tail = summed(main, TAIL)
    bias = tail[0:1] + tail[1:2]
    high = bias.astype(BF).astype(F32)
    for r, value in enumerate((high, bias - high)):
        full = jnp.broadcast_to(value, (h_n * l_n, LANES))
        spread[pl.ds(lines + r, h_n * l_n, stride=group), :] = full
    out_ref[...] = spread[...].astype(BF)


def line_kernel(lines, part_ref, back_ref, out_ref):
    total = part_ref[0].astype(F32)
    for p in range(1, part_ref.shape[0]):
        total = total + part_ref[p].astype(F32)
    group = total.shape[0]
    row = iota((group, LANES), 0)
    bias = total[lines : lines + 1] + total[lines + 1 : lines + 2]
    high = bias.astype(BF).astype(F32)
    total = jnp.where(row == lines, high, jnp.where(row == lines + 1, bias - high, total))
    for p in range(out_ref.shape[0]):
        value = back_ref[p : p + 1, :]
        head = value.astype(BF).astype(F32)
        tile = jnp.where(row == group - 2, head, jnp.where(row == group - 1, value - head, total))
        out_ref[p] = tile.astype(BF)


def unpack_kernel(
    dims, back_ref, own_ref, both_ref, order_ref, cos_ref, weight_ref, bias_ref, wide, narrow
):
    y_n, h_n, x_n, l_n, c_n, two = dims
    near, per = x_n * l_n, c_n * two
    group = own_ref.shape[0] // near
    wide[...] = both_ref[...].astype(F32)
    narrow[...] = own_ref[...].astype(F32)
    half = weight_ref.shape[1] // c_n
    pairs = half // LANES
    lines = pairs * LINE_ROWS
    for c in range(c_n):
        for x in range(x_n):
            for k in range(pairs):
                for r in range(LINE_ROWS):
                    start = (c * near + x * l_n) * group + k * LINE_ROWS + r
                    to = (x * LINE_ROWS + r) * l_n
                    at = c * half + k * LANES
                    weight_ref[to : to + l_n, at : at + LANES] = wide[pl.ds(start, l_n, stride=group), :]
    cosines = narrow[pl.ds(group - 2, near, stride=group), :] + narrow[pl.ds(group - 1, near, stride=group), :]
    order = order_ref[...]
    tokens = order.shape[1]
    base = iota((near, tokens), 0) * per
    total = jnp.zeros((near, tokens), F32)
    for i in range(per):
        total = total + jnp.where(order == base + i, cosines[:, i : i + 1], 0.0)
    cos_ref[...] = jnp.sum(total, axis=0, keepdims=True)
    cols = bias_ref.shape[1]
    blocks = cols * h_n // LANES
    offset = back_ref[near:, :cols].astype(I32)[0:1] * cols
    out = jnp.zeros((8, cols), F32)
    for b in range(blocks):
        start = b * l_n * group + lines
        pick = iota((LANES, cols), 0) + b * LANES == iota((LANES, cols), 1) + offset
        pick = jnp.where(pick, 1.0, 0.0).astype(BF)
        for r in range(2):
            term = jnp.broadcast_to(narrow[start + r : start + r + 1, :], (8, LANES)).astype(BF)
            out = out + jnp.dot(term, pick, preferred_element_type=F32)
    bias_ref[...] = out[0:1]


def local(hidden, weight, bias, patches, slots, order, cotangent):
    y_n, h_n, x_n, l_n, c_n = (lax.axis_size(a) for a in ("y", "h", "x", "l", "c"))
    patches = patches[0]
    tokens, units = hidden.shape[1:]
    width = weight.shape[1]
    near = x_n * l_n
    per = tokens // near
    shards = near * c_n
    two = tokens // shards
    half = width // c_n
    dims = (y_n, h_n, x_n, l_n, c_n, two)
    shape = jax.ShapeDtypeStruct
    core = lax.axis_index("c").astype(I32)[None]
    high = lax.axis_index("h").astype(I32)[None]

    sent = call(send_kernel, shape((near, per, units + LANES), BF), [VMEM] * 3, limit=60)(
        hidden[0], order, cotangent
    )
    moved = lax.all_to_all(sent, ("x", "l"), 0, 0, tiled=True)
    pooled = call(
        functools.partial(pool_kernel, dims), shape((tokens, width), BF), [VMEM] * 2, limit=60
    )(patches, slots)
    pooled = lax.all_gather(pooled, "c", axis=0, tiled=True)
    pooled = pltpu.with_memory_space_constraint(pooled, pltpu.HBM)

    both = lax.all_gather(moved, "c", axis=0, tiled=True)
    rows = units // (y_n * x_n)
    lines = half // LANES * LINE_ROWS
    part, back = call(
        functools.partial(middle_kernel, dims),
        (
            shape((y_n * x_n, rows * half // LANES + TAIL, LANES), BF),
            shape((near + 8, LANES), F32),
        ),
        [SMEM] * 2 + [VMEM, pl.BlockSpec(memory_space=pltpu.HBM), VMEM, VMEM],
        [
            pltpu.VMEM((c_n * tokens, width), F32),
            pltpu.VMEM((c_n * tokens, width), F32),
            pltpu.VMEM((c_n, c_n * tokens, half), BF),
            pltpu.VMEM((c_n * tokens, units + LANES), F32),
            pltpu.VMEM((c_n * tokens, units), BF),
            pltpu.VMEM((c_n * tokens, width), BF),
            pltpu.SemaphoreType.DMA,
        ],
    )(core, high, both, pooled, weight, bias[None, :])

    part = lax.all_to_all(part, ("y", "x"), 0, 0, tiled=True)
    spots = h_n * l_n
    part = call(
        functools.partial(plane_kernel, dims),
        shape((spots * TAIL, LANES), BF),
        [VMEM],
        [pltpu.VMEM((spots * TAIL, LANES), F32)],
    )(part)
    part, back = lax.optimization_barrier((part, back))
    part = lax.all_to_all(part.reshape(spots, TAIL, LANES), ("h", "l"), 0, 0, tiled=True)
    part = call(functools.partial(line_kernel, lines), shape((near, TAIL, LANES), BF), [VMEM] * 2)(part, back)
    part = lax.all_to_all(part, ("x", "l"), 0, 0, tiled=True).reshape(near * TAIL, LANES)
    wide = lax.all_gather(part, "c", axis=0, tiled=True)
    cos_sim, weight_grad, bias_grad = call(
        functools.partial(unpack_kernel, dims),
        (
            shape((1, tokens), F32),
            shape((units // (y_n * h_n), width), F32),
            shape((1, width // (y_n * h_n)), F32),
        ),
        [VMEM] * 4,
        [pltpu.VMEM((c_n * near * TAIL, LANES), F32), pltpu.VMEM((near * TAIL, LANES), F32)],
    )(back, part, wide, order)
    return cos_sim, weight_grad, bias_grad[0]


def solution(mesh, sizes=(4, 4, 4, 8, 2)):
    fine = Mesh(mesh.devices.reshape(sizes), ("y", "h", "x", "l", "c"))
    clip, seq = ("y", "h"), ("x", "l", "c")
    placed = (
        P(clip, seq, None),
        P(),
        P(),
        P(clip, seq, None),
        P(clip, seq),
        P(clip, seq),
        P(clip, seq),
    )
    return jax.shard_map(
        local,
        mesh=fine,
        in_specs=placed,
        out_specs=(P(clip, seq), P(clip, None), P(clip)),
        check_vma=False,
    )
```

```python
import functools

import jax
import jax.numpy as jnp
from jax import lax
from jax.experimental import pallas as pl
from jax.experimental.pallas import tpu as pltpu
from jax.sharding import Mesh, PartitionSpec as P

BF = jnp.bfloat16
F32 = jnp.float32
I32 = jnp.int32
LANES = 128
TAIL = 16
LINE_ROWS = 2
VMEM = pl.BlockSpec(memory_space=pltpu.VMEM)
SMEM = pl.BlockSpec(memory_space=pltpu.SMEM)


def iota(shape, axis):
    return lax.broadcasted_iota(I32, shape, axis)


def split_two(values):
    head = values.astype(BF)
    return head, (values - head.astype(F32)).astype(BF)


def call(body, outs, ins, scratch=(), limit=16):
    return pl.pallas_call(
        body,
        out_shape=outs,
        in_specs=ins,
        out_specs=jax.tree.map(lambda _: VMEM, outs),
        scratch_shapes=list(scratch),
        compiler_params=pltpu.CompilerParams(vmem_limit_bytes=limit << 20),
    )


def send_kernel(hidden_ref, order_ref, cot_ref, out_ref):
    tokens, units = hidden_ref.shape
    pieces, per = out_ref.shape[:2]
    pick = order_ref[...] == iota((tokens, tokens), 0)
    rows = jnp.dot(
        jnp.where(pick, 1.0, 0.0).astype(BF), hidden_ref[...], preferred_element_type=F32
    )
    cot = jnp.sum(jnp.where(pick, cot_ref[...], 0.0), axis=1, keepdims=True)
    high = cot.astype(BF).astype(F32)
    rest = cot - high
    middle = rest.astype(BF).astype(F32)
    low = rest - middle
    lane = iota((tokens, LANES), 1)
    cols = jnp.where(lane == 0, high, jnp.where(lane == 1, middle, jnp.where(lane == 2, low, 0.0)))
    for p in range(pieces):
        at = slice(p * per, (p + 1) * per)
        out_ref[p] = jnp.concatenate([rows[at], cols[at]], axis=1).astype(BF)


def pool_kernel(dims, patch_ref, slot_ref, pooled_ref):
    y_n, h_n, x_n, l_n, c_n, two = dims
    tokens, patches = pooled_ref.shape[0], patch_ref.shape[0]
    shape = (tokens, patches)
    row = iota(shape, 0)
    near = x_n * l_n
    src = row // two % near * c_n + row // (near * two)
    match = (iota(shape, 1) // (patches // (near * c_n)) == src) & (slot_ref[...] == row % two)
    match = jnp.where(match, 1.0, 0.0)
    counts = jnp.sum(match, axis=1, keepdims=True)
    totals = jnp.dot(match.astype(BF), patch_ref[...], preferred_element_type=F32)
    pooled_ref[...] = (totals / counts).astype(BF)


def middle_kernel(
    dims, core_ref, high_ref, both_ref, pooled_ref, weight_ref, bias_ref, part_ref, back_ref,
    proj, target, grads, terms, acts, pooled, sem
):
    y_n, h_n, x_n, l_n, c_n, two = dims
    near, per = x_n * l_n, c_n * two
    tokens, units = acts.shape
    fetch = pltpu.make_async_copy(pooled_ref, pooled, sem)
    fetch.start()
    join = TAIL // per
    for g in range(tokens // TAIL):
        tall = jnp.concatenate([both_ref[g * join + i].astype(F32) for i in range(join)], axis=0)
        at = slice(g * TAIL, (g + 1) * TAIL)
        acts[at, :] = tall[:, :units].astype(BF)
        terms[at, :] = tall[:, units:]
    width = weight_ref.shape[1]
    half = width // c_n
    single = tokens // c_n
    core = core_ref[0]
    row = iota((tokens, tokens), 0)
    wanted = (
        (row // two) % c_n * single + row // single * (near * two) + row // per % near * two + row % two
    )
    turn = jnp.where(wanted == iota((tokens, tokens), 1), 1.0, 0.0).astype(BF)
    step = 256
    s_pp = jnp.zeros((tokens, 1), F32)
    s_tt = jnp.zeros((tokens, 1), F32)
    s_pt = jnp.zeros((tokens, 1), F32)
    for at in range(0, width, step):
        cut = slice(at, at + step)
        p = jnp.dot(acts[...], weight_ref[:, cut], preferred_element_type=F32) + bias_ref[:, cut]
        proj[:, cut] = p
        s_pp = s_pp + jnp.sum(p * p, axis=1, keepdims=True)
    fetch.wait()
    for at in range(0, width, step):
        cut = slice(at, at + step)
        t = jnp.dot(turn, pooled[:, cut], preferred_element_type=F32)
        target[:, cut] = t
        s_tt = s_tt + jnp.sum(t * t, axis=1, keepdims=True)
        s_pt = s_pt + jnp.sum(proj[:, cut] * t, axis=1, keepdims=True)
    inv_proj = lax.rsqrt(s_pp + 1e-06)
    inv_target = lax.rsqrt(s_tt + 1e-06)
    cosine = s_pt * inv_proj * inv_target
    cot = (terms[:, 2:3] + terms[:, 1:2]) + terms[:, 0:1]
    scale_t = inv_proj * inv_target
    scale_p = cosine * inv_proj * inv_proj
    y_blocks = width // y_n // LANES
    tail_row = iota((TAIL, step), 0)
    main = part_ref.shape[1] - TAIL
    for at in range(0, width, step):
        g = cot * (target[:, at : at + step] * scale_t - scale_p * proj[:, at : at + step])
        g = g.astype(BF)
        inside = at % half
        grads[at // half, :, inside : inside + step] = g
        total = jnp.sum(g.astype(F32), axis=0, keepdims=True)
        high = total.astype(BF).astype(F32)
        tail = jnp.where(tail_row == 0, high, jnp.where(tail_row == 1, total - high, 0.0)).astype(BF)
        for k in range(step // LANES):
            block = at // LANES + k
            piece = block % y_blocks * y_n + block // y_blocks
            part_ref[piece, main:, :] = tail[:, k * LANES : (k + 1) * LANES]
    for y in range(y_n):
        for x in range(y_blocks, x_n):
            part_ref[x * y_n + y, main:, :] = jnp.zeros((TAIL, LANES), BF)
    lane = iota((tokens, LANES), 1)
    high, low = split_two(cosine)
    spot = iota((tokens, LANES), 0) % per == lane
    owner = iota((near, tokens), 1) - core * single
    gather = jnp.where((owner >= 0) & (owner < single) & (owner // per == iota((near, tokens), 0)), 1.0, 0.0)
    gather = gather.astype(BF)
    back = jnp.zeros((near, LANES), F32)
    for term in (high, low):
        spread = jnp.where(spot, term.astype(F32), 0.0).astype(BF)
        back = back + jnp.dot(gather, spread, preferred_element_type=F32)
    back_ref[:near, :] = back
    back_ref[near:, :] = jnp.full((8, LANES), high_ref[0], I32).astype(F32)
    rows = units // y_n
    chunk = rows // h_n // x_n
    mine = grads[core]
    for y in range(y_n):
        product = lax.dot_general(
            acts[:, y * rows : (y + 1) * rows], mine, (((0,), (0,)), ((), ())), preferred_element_type=F32
        ).astype(BF)
        for h in range(h_n):
            for x in range(x_n):
                start = (h * x_n + x) * chunk
                for k in range(half // LANES):
                    to = (k * h_n + h) * chunk
                    part_ref[x * y_n + y, to : to + chunk, :] = product[
                        start : start + chunk, k * LANES : (k + 1) * LANES
                    ]


def plane_kernel(dims, part_ref, out_ref, spread):
    y_n, h_n, x_n, l_n, c_n, two = dims
    count, total_rows = part_ref.shape[0], part_ref.shape[1]
    main = total_rows - TAIL
    spread[...] = jnp.zeros_like(spread)
    group = out_ref.shape[0] // (h_n * l_n)
    lines = main // (h_n * l_n)

    def summed(start, size):
        total = part_ref[0, start : start + size, :].astype(F32)
        for p in range(1, count):
            total = total + part_ref[p, start : start + size, :].astype(F32)
        return total

    pair = lines // LINE_ROWS
    size = h_n * LINE_ROWS * l_n
    for k in range(pair):
        total = summed(k * size, size)
        for h in range(h_n):
            for r in range(LINE_ROWS):
                at = (h * LINE_ROWS + r) * l_n
                spread[pl.ds(h * group + k * LINE_ROWS + r, l_n, stride=h_n * group), :] = total[at : at + l_n]
    tail = summed(main, TAIL)
    bias = tail[0:1] + tail[1:2]
    high = bias.astype(BF).astype(F32)
    for r, value in enumerate((high, bias - high)):
        full = jnp.broadcast_to(value, (h_n * l_n, LANES))
        spread[pl.ds(lines + r, h_n * l_n, stride=group), :] = full
    out_ref[...] = spread[...].astype(BF)


def line_kernel(lines, part_ref, back_ref, out_ref):
    total = part_ref[0].astype(F32)
    for p in range(1, part_ref.shape[0]):
        total = total + part_ref[p].astype(F32)
    group = total.shape[0]
    row = iota((group, LANES), 0)
    bias = total[lines : lines + 1] + total[lines + 1 : lines + 2]
    high = bias.astype(BF).astype(F32)
    total = jnp.where(row == lines, high, jnp.where(row == lines + 1, bias - high, total))
    for p in range(out_ref.shape[0]):
        value = back_ref[p : p + 1, :]
        head = value.astype(BF).astype(F32)
        tile = jnp.where(row == group - 2, head, jnp.where(row == group - 1, value - head, total))
        out_ref[p] = tile.astype(BF)


def unpack_kernel(
    dims, back_ref, own_ref, both_ref, order_ref, cos_ref, weight_ref, bias_ref, wide, narrow
):
    y_n, h_n, x_n, l_n, c_n, two = dims
    near, per = x_n * l_n, c_n * two
    group = own_ref.shape[0] // near
    wide[...] = both_ref[...].astype(F32)
    narrow[...] = own_ref[...].astype(F32)
    half = weight_ref.shape[1] // c_n
    pairs = half // LANES
    lines = pairs * LINE_ROWS
    for c in range(c_n):
        for x in range(x_n):
            for k in range(pairs):
                for r in range(LINE_ROWS):
                    start = (c * near + x * l_n) * group + k * LINE_ROWS + r
                    to = (x * LINE_ROWS + r) * l_n
                    at = c * half + k * LANES
                    weight_ref[to : to + l_n, at : at + LANES] = wide[pl.ds(start, l_n, stride=group), :]
    cosines = narrow[pl.ds(group - 2, near, stride=group), :] + narrow[pl.ds(group - 1, near, stride=group), :]
    order = order_ref[...]
    tokens = order.shape[1]
    base = iota((near, tokens), 0) * per
    total = jnp.zeros((near, tokens), F32)
    for i in range(per):
        total = total + jnp.where(order == base + i, cosines[:, i : i + 1], 0.0)
    cos_ref[...] = jnp.sum(total, axis=0, keepdims=True)
    cols = bias_ref.shape[1]
    blocks = cols * h_n // LANES
    offset = back_ref[near:, :cols].astype(I32)[0:1] * cols
    out = jnp.zeros((8, cols), F32)
    for b in range(blocks):
        start = b * l_n * group + lines
        pick = iota((LANES, cols), 0) + b * LANES == iota((LANES, cols), 1) + offset
        pick = jnp.where(pick, 1.0, 0.0).astype(BF)
        for r in range(2):
            term = jnp.broadcast_to(narrow[start + r : start + r + 1, :], (8, LANES)).astype(BF)
            out = out + jnp.dot(term, pick, preferred_element_type=F32)
    bias_ref[...] = out[0:1]


def local(hidden, weight, bias, patches, slots, order, cotangent):
    y_n, h_n, x_n, l_n, c_n = (lax.axis_size(a) for a in ("y", "h", "x", "l", "c"))
    patches = patches[0]
    tokens, units = hidden.shape[1:]
    width = weight.shape[1]
    near = x_n * l_n
    per = tokens // near
    shards = near * c_n
    two = tokens // shards
    half = width // c_n
    dims = (y_n, h_n, x_n, l_n, c_n, two)
    shape = jax.ShapeDtypeStruct
    core = lax.axis_index("c").astype(I32)[None]
    high = lax.axis_index("h").astype(I32)[None]

    sent = call(send_kernel, shape((near, per, units + LANES), BF), [VMEM] * 3, limit=60)(
        hidden[0], order, cotangent
    )
    moved = lax.all_to_all(sent, ("x", "l"), 0, 0, tiled=True)
    pooled = call(
        functools.partial(pool_kernel, dims), shape((tokens, width), BF), [VMEM] * 2, limit=60
    )(patches, slots)
    pooled = lax.all_gather(pooled, "c", axis=0, tiled=True)
    pooled = pltpu.with_memory_space_constraint(pooled, pltpu.HBM)

    both = lax.all_gather(moved, "c", axis=0, tiled=True)
    rows = units // (y_n * x_n)
    lines = half // LANES * LINE_ROWS
    part, back = call(
        functools.partial(middle_kernel, dims),
        (
            shape((y_n * x_n, rows * half // LANES + TAIL, LANES), BF),
            shape((near + 8, LANES), F32),
        ),
        [SMEM] * 2 + [VMEM, pl.BlockSpec(memory_space=pltpu.HBM), VMEM, VMEM],
        [
            pltpu.VMEM((c_n * tokens, width), F32),
            pltpu.VMEM((c_n * tokens, width), F32),
            pltpu.VMEM((c_n, c_n * tokens, half), BF),
            pltpu.VMEM((c_n * tokens, LANES), F32),
            pltpu.VMEM((c_n * tokens, units), BF),
            pltpu.VMEM((c_n * tokens, width), BF),
            pltpu.SemaphoreType.DMA,
        ],
    )(core, high, both, pooled, weight, bias[None, :])

    part = lax.all_to_all(part, ("x", "y"), 0, 0, tiled=True)
    spots = h_n * l_n
    part = call(
        functools.partial(plane_kernel, dims),
        shape((spots * TAIL, LANES), BF),
        [VMEM],
        [pltpu.VMEM((spots * TAIL, LANES), F32)],
    )(part)
    part, back = lax.optimization_barrier((part, back))
    part = lax.all_to_all(part.reshape(spots, TAIL, LANES), ("l", "h"), 0, 0, tiled=True)
    part = call(functools.partial(line_kernel, lines), shape((near, TAIL, LANES), BF), [VMEM] * 2)(part, back)
    part = lax.all_to_all(part, ("x", "l"), 0, 0, tiled=True).reshape(near * TAIL, LANES)
    wide = lax.all_gather(part, "c", axis=0, tiled=True)
    cos_sim, weight_grad, bias_grad = call(
        functools.partial(unpack_kernel, dims),
        (
            shape((1, tokens), F32),
            shape((units // (y_n * h_n), width), F32),
            shape((1, width // (y_n * h_n)), F32),
        ),
        [VMEM] * 4,
        [pltpu.VMEM((c_n * near * TAIL, LANES), F32), pltpu.VMEM((near * TAIL, LANES), F32)],
    )(back, part, wide, order)
    return cos_sim, weight_grad, bias_grad[0]


def solution(mesh, sizes=(4, 4, 4, 8, 2)):
    fine = Mesh(mesh.devices.reshape(sizes), ("y", "h", "x", "l", "c"))
    clip, seq = ("y", "h"), ("x", "l", "c")
    placed = (
        P(clip, seq, None),
        P(),
        P(),
        P(clip, seq, None),
        P(clip, seq),
        P(clip, seq),
        P(clip, seq),
    )
    return jax.shard_map(
        local,
        mesh=fine,
        in_specs=placed,
        out_specs=(P(clip, seq), P(clip, None), P(clip)),
        check_vma=False,
    )
```

```python
import functools

import jax
import jax.numpy as jnp
from jax import lax
from jax.experimental import pallas as pl
from jax.experimental.pallas import tpu as pltpu
from jax.sharding import Mesh, PartitionSpec as P

BF = jnp.bfloat16
F32 = jnp.float32
I32 = jnp.int32
LANES = 128
TAIL = 16
LINE_ROWS = 2
VMEM = pl.BlockSpec(memory_space=pltpu.VMEM)
SMEM = pl.BlockSpec(memory_space=pltpu.SMEM)
HBM = pl.BlockSpec(memory_space=pltpu.HBM)


def iota(shape, axis):
    return lax.broadcasted_iota(I32, shape, axis)


def split_two(values):
    head = values.astype(BF)
    return head, (values - head.astype(F32)).astype(BF)


def call(body, outs, ins, scratch=(), limit=16):
    return pl.pallas_call(
        body,
        out_shape=outs,
        in_specs=ins,
        out_specs=jax.tree.map(lambda _: VMEM, outs),
        scratch_shapes=list(scratch),
        compiler_params=pltpu.CompilerParams(vmem_limit_bytes=limit << 20),
    )


def send_kernel(hidden_ref, order_ref, cot_ref, out_ref):
    tokens, units = hidden_ref.shape
    pieces, per = out_ref.shape[:2]
    pick = order_ref[...] == iota((tokens, tokens), 0)
    rows = jnp.dot(
        jnp.where(pick, 1.0, 0.0).astype(BF), hidden_ref[...], preferred_element_type=F32
    )
    cot = jnp.sum(jnp.where(pick, cot_ref[...], 0.0), axis=1, keepdims=True)
    high = cot.astype(BF).astype(F32)
    rest = cot - high
    middle = rest.astype(BF).astype(F32)
    low = rest - middle
    lane = iota((tokens, LANES), 1)
    cols = jnp.where(lane == 0, high, jnp.where(lane == 1, middle, jnp.where(lane == 2, low, 0.0)))
    for p in range(pieces):
        at = slice(p * per, (p + 1) * per)
        out_ref[p] = jnp.concatenate([rows[at], cols[at]], axis=1).astype(BF)


def pool_kernel(dims, patch_ref, slot_ref, pooled_ref):
    y_n, h_n, x_n, l_n, c_n, two = dims
    tokens, patches = pooled_ref.shape[0], patch_ref.shape[0]
    shape = (tokens, patches)
    row = iota(shape, 0)
    near = x_n * l_n
    src = row // two % near * c_n + row // (near * two)
    match = (iota(shape, 1) // (patches // (near * c_n)) == src) & (slot_ref[...] == row % two)
    match = jnp.where(match, 1.0, 0.0)
    counts = jnp.sum(match, axis=1, keepdims=True)
    totals = jnp.dot(match.astype(BF), patch_ref[...], preferred_element_type=F32)
    pooled_ref[...] = (totals / counts).astype(BF)


def middle_kernel(
    dims, core_ref, high_ref, both_ref, pooled_ref, weight_ref, rest_ref, bias_ref, part_ref, back_ref,
    proj, target, grads, held, pooled, sems
):
    y_n, h_n, x_n, l_n, c_n, two = dims
    near, per = x_n * l_n, c_n * two
    tokens, units = both_ref.shape[0], both_ref.shape[1] - LANES
    first = weight_ref.shape[1]
    fetch_rest = pltpu.make_async_copy(rest_ref.at[:, pl.ds(first, LANES)], held, sems.at[1])
    fetch_rest.start()
    fetch = pltpu.make_async_copy(pooled_ref, pooled, sems.at[0])
    fetch.start()
    acts = both_ref[:, :units]
    width = rest_ref.shape[1]
    half = width // c_n
    single = tokens // c_n
    core = core_ref[0]
    row = iota((tokens, tokens), 0)
    wanted = (
        (row // two) % c_n * single + row // single * (near * two) + row // per % near * two + row % two
    )
    turn = jnp.where(wanted == iota((tokens, tokens), 1), 1.0, 0.0).astype(BF)
    step = 256
    s_pp = jnp.zeros((tokens, 1), F32)
    s_tt = jnp.zeros((tokens, 1), F32)
    s_pt = jnp.zeros((tokens, 1), F32)
    starts = list(range(0, first - step + 1, step))
    blocks = [(at, step) for at in starts] + [(at, LANES) for at in range(len(starts) * step, width, LANES)]
    for at, size in blocks:
        cut = slice(at, at + size)
        if at == first:
            fetch_rest.wait()
        block = held[...] if at == first else weight_ref[:, cut]
        p = jnp.dot(acts, block, preferred_element_type=F32) + bias_ref[:, cut]
        proj[:, cut] = p
        s_pp = s_pp + jnp.sum(p * p, axis=1, keepdims=True)
    fetch.wait()
    for at in range(0, width, step):
        cut = slice(at, at + step)
        t = jnp.dot(turn, pooled[:, cut], preferred_element_type=F32)
        target[:, cut] = t
        s_tt = s_tt + jnp.sum(t * t, axis=1, keepdims=True)
        s_pt = s_pt + jnp.sum(proj[:, cut] * t, axis=1, keepdims=True)
    inv_proj = lax.rsqrt(s_pp + 1e-06)
    inv_target = lax.rsqrt(s_tt + 1e-06)
    cosine = s_pt * inv_proj * inv_target
    terms = both_ref[:, units:].astype(F32)
    cot = (terms[:, 2:3] + terms[:, 1:2]) + terms[:, 0:1]
    scale_t = inv_proj * inv_target
    scale_p = cosine * inv_proj * inv_proj
    y_blocks = width // y_n // LANES
    tail_row = iota((TAIL, step), 0)
    main = part_ref.shape[1] - TAIL
    for at in range(0, width, step):
        g = cot * (target[:, at : at + step] * scale_t - scale_p * proj[:, at : at + step])
        g = g.astype(BF)
        inside = at % half
        grads[at // half, :, inside : inside + step] = g
        total = jnp.sum(g.astype(F32), axis=0, keepdims=True)
        high = total.astype(BF).astype(F32)
        tail = jnp.where(tail_row == 0, high, jnp.where(tail_row == 1, total - high, 0.0)).astype(BF)
        for k in range(step // LANES):
            block = at // LANES + k
            piece = block % y_blocks * y_n + block // y_blocks
            part_ref[piece, main:, :] = tail[:, k * LANES : (k + 1) * LANES]
    for y in range(y_n):
        for x in range(y_blocks, x_n):
            part_ref[x * y_n + y, main:, :] = jnp.zeros((TAIL, LANES), BF)
    lane = iota((tokens, LANES), 1)
    high, low = split_two(cosine)
    spot = iota((tokens, LANES), 0) % per == lane
    owner = iota((near, tokens), 1) - core * single
    gather = jnp.where((owner >= 0) & (owner < single) & (owner // per == iota((near, tokens), 0)), 1.0, 0.0)
    gather = gather.astype(BF)
    back = jnp.zeros((near, LANES), F32)
    for term in (high, low):
        spread = jnp.where(spot, term.astype(F32), 0.0).astype(BF)
        back = back + jnp.dot(gather, spread, preferred_element_type=F32)
    back_ref[:near, :] = back
    back_ref[near:, :] = jnp.full((8, LANES), high_ref[0], I32).astype(F32)
    rows = units // y_n
    chunk = rows // h_n // x_n
    mine = grads[core]
    for y in range(y_n):
        product = lax.dot_general(
            acts[:, y * rows : (y + 1) * rows], mine, (((0,), (0,)), ((), ())), preferred_element_type=F32
        ).astype(BF)
        for h in range(h_n):
            for x in range(x_n):
                start = (h * x_n + x) * chunk
                for k in range(half // LANES):
                    to = (k * h_n + h) * chunk
                    part_ref[x * y_n + y, to : to + chunk, :] = product[
                        start : start + chunk, k * LANES : (k + 1) * LANES
                    ]


def plane_kernel(dims, part_ref, out_ref, spread):
    y_n, h_n, x_n, l_n, c_n, two = dims
    count, total_rows = part_ref.shape[0], part_ref.shape[1]
    main = total_rows - TAIL
    spread[...] = jnp.zeros_like(spread)
    group = out_ref.shape[0] // (h_n * l_n)
    lines = main // (h_n * l_n)

    def summed(start, size):
        total = part_ref[0, start : start + size, :].astype(F32)
        for p in range(1, count):
            total = total + part_ref[p, start : start + size, :].astype(F32)
        return total

    pair = lines // LINE_ROWS
    size = h_n * LINE_ROWS * l_n
    for k in range(pair):
        total = summed(k * size, size)
        for h in range(h_n):
            for r in range(LINE_ROWS):
                at = (h * LINE_ROWS + r) * l_n
                spread[pl.ds(h * group + k * LINE_ROWS + r, l_n, stride=h_n * group), :] = total[at : at + l_n]
    tail = summed(main, TAIL)
    bias = tail[0:1] + tail[1:2]
    high = bias.astype(BF).astype(F32)
    for r, value in enumerate((high, bias - high)):
        full = jnp.broadcast_to(value, (h_n * l_n, LANES))
        spread[pl.ds(lines + r, h_n * l_n, stride=group), :] = full
    out_ref[...] = spread[...].astype(BF)


def line_kernel(lines, part_ref, back_ref, out_ref):
    total = part_ref[0].astype(F32)
    for p in range(1, part_ref.shape[0]):
        total = total + part_ref[p].astype(F32)
    group = total.shape[0]
    row = iota((group, LANES), 0)
    bias = total[lines : lines + 1] + total[lines + 1 : lines + 2]
    high = bias.astype(BF).astype(F32)
    total = jnp.where(row == lines, high, jnp.where(row == lines + 1, bias - high, total))
    for p in range(out_ref.shape[0]):
        value = back_ref[p : p + 1, :]
        head = value.astype(BF).astype(F32)
        tile = jnp.where(row == group - 2, head, jnp.where(row == group - 1, value - head, total))
        out_ref[p] = tile.astype(BF)


def unpack_kernel(
    dims, back_ref, own_ref, both_ref, order_ref, cos_ref, weight_ref, bias_ref, wide, narrow
):
    y_n, h_n, x_n, l_n, c_n, two = dims
    near, per = x_n * l_n, c_n * two
    group = own_ref.shape[0] // near
    wide[...] = both_ref[...].astype(F32)
    narrow[...] = own_ref[...].astype(F32)
    half = weight_ref.shape[1] // c_n
    pairs = half // LANES
    lines = pairs * LINE_ROWS
    for c in range(c_n):
        for x in range(x_n):
            for k in range(pairs):
                for r in range(LINE_ROWS):
                    start = (c * near + x * l_n) * group + k * LINE_ROWS + r
                    to = (x * LINE_ROWS + r) * l_n
                    at = c * half + k * LANES
                    weight_ref[to : to + l_n, at : at + LANES] = wide[pl.ds(start, l_n, stride=group), :]
    cosines = narrow[pl.ds(group - 2, near, stride=group), :] + narrow[pl.ds(group - 1, near, stride=group), :]
    order = order_ref[...]
    tokens = order.shape[1]
    base = iota((near, tokens), 0) * per
    total = jnp.zeros((near, tokens), F32)
    for i in range(per):
        total = total + jnp.where(order == base + i, cosines[:, i : i + 1], 0.0)
    cos_ref[...] = jnp.sum(total, axis=0, keepdims=True)
    cols = bias_ref.shape[1]
    blocks = cols * h_n // LANES
    offset = back_ref[near:, :cols].astype(I32)[0:1] * cols
    out = jnp.zeros((8, cols), F32)
    for b in range(blocks):
        start = b * l_n * group + lines
        pick = iota((LANES, cols), 0) + b * LANES == iota((LANES, cols), 1) + offset
        pick = jnp.where(pick, 1.0, 0.0).astype(BF)
        for r in range(2):
            term = jnp.broadcast_to(narrow[start + r : start + r + 1, :], (8, LANES)).astype(BF)
            out = out + jnp.dot(term, pick, preferred_element_type=F32)
    bias_ref[...] = out[0:1]


def local(hidden, weight, bias, patches, slots, order, cotangent):
    y_n, h_n, x_n, l_n, c_n = (lax.axis_size(a) for a in ("y", "h", "x", "l", "c"))
    patches = patches[0]
    tokens, units = hidden.shape[1:]
    width = weight.shape[1]
    near = x_n * l_n
    per = tokens // near
    shards = near * c_n
    two = tokens // shards
    half = width // c_n
    dims = (y_n, h_n, x_n, l_n, c_n, two)
    shape = jax.ShapeDtypeStruct
    core = lax.axis_index("c").astype(I32)[None]
    high = lax.axis_index("h").astype(I32)[None]

    sent = call(send_kernel, shape((near, per, units + LANES), BF), [VMEM] * 3, limit=60)(
        hidden[0], order, cotangent
    )
    moved = lax.all_to_all(sent, ("x", "l"), 0, 0, tiled=True)
    pooled = call(
        functools.partial(pool_kernel, dims), shape((tokens, width), BF), [VMEM] * 2, limit=60
    )(patches, slots)
    pooled = lax.all_gather(pooled, "c", axis=0, tiled=True)
    pooled = pltpu.with_memory_space_constraint(pooled, pltpu.HBM)

    both = lax.all_gather(moved.reshape(tokens, units + LANES), "c", axis=0, tiled=True)
    rows = units // (y_n * x_n)
    lines = half // LANES * LINE_ROWS
    part, back = call(
        functools.partial(middle_kernel, dims),
        (
            shape((y_n * x_n, rows * half // LANES + TAIL, LANES), BF),
            shape((near + 8, LANES), F32),
        ),
        [SMEM] * 2 + [VMEM, HBM, VMEM, HBM, VMEM],
        [
            pltpu.VMEM((c_n * tokens, width), F32),
            pltpu.VMEM((c_n * tokens, width), F32),
            pltpu.VMEM((c_n, c_n * tokens, half), BF),
            pltpu.VMEM((units, LANES), BF),
            pltpu.VMEM((c_n * tokens, width), BF),
            pltpu.SemaphoreType.DMA((2,)),
        ],
    )(core, high, both, pooled, weight[:, : width - LANES], pltpu.with_memory_space_constraint(weight, pltpu.HBM), bias[None, :])

    part = lax.all_to_all(part, ("x", "y"), 0, 0, tiled=True)
    spots = h_n * l_n
    part = call(
        functools.partial(plane_kernel, dims),
        shape((spots * TAIL, LANES), BF),
        [VMEM],
        [pltpu.VMEM((spots * TAIL, LANES), F32)],
    )(part)
    part, back = lax.optimization_barrier((part, back))
    part = lax.all_to_all(part.reshape(spots, TAIL, LANES), ("l", "h"), 0, 0, tiled=True)
    part = call(functools.partial(line_kernel, lines), shape((near, TAIL, LANES), BF), [VMEM] * 2)(part, back)
    part = lax.all_to_all(part, ("x", "l"), 0, 0, tiled=True).reshape(near * TAIL, LANES)
    wide = lax.all_gather(part, "c", axis=0, tiled=True)
    cos_sim, weight_grad, bias_grad = call(
        functools.partial(unpack_kernel, dims),
        (
            shape((1, tokens), F32),
            shape((units // (y_n * h_n), width), F32),
            shape((1, width // (y_n * h_n)), F32),
        ),
        [VMEM] * 4,
        [pltpu.VMEM((c_n * near * TAIL, LANES), F32), pltpu.VMEM((near * TAIL, LANES), F32)],
    )(back, part, wide, order)
    return cos_sim, weight_grad, bias_grad[0]


def solution(mesh, sizes=(4, 4, 4, 8, 2)):
    fine = Mesh(mesh.devices.reshape(sizes), ("y", "h", "x", "l", "c"))
    clip, seq = ("y", "h"), ("x", "l", "c")
    placed = (
        P(clip, seq, None),
        P(),
        P(),
        P(clip, seq, None),
        P(clip, seq),
        P(clip, seq),
        P(clip, seq),
    )
    return jax.shard_map(
        local,
        mesh=fine,
        in_specs=placed,
        out_specs=(P(clip, seq), P(clip, None), P(clip)),
        check_vma=False,
    )
```

```python
import functools

import jax
import jax.numpy as jnp
from jax import lax
from jax.experimental import pallas as pl
from jax.experimental.pallas import tpu as pltpu
from jax.sharding import Mesh, PartitionSpec as P

BF = jnp.bfloat16
F32 = jnp.float32
I32 = jnp.int32
LANES = 128
TAIL = 16
LINE_ROWS = 2
VMEM = pl.BlockSpec(memory_space=pltpu.VMEM)
SMEM = pl.BlockSpec(memory_space=pltpu.SMEM)
HBM = pl.BlockSpec(memory_space=pltpu.HBM)


def iota(shape, axis):
    return lax.broadcasted_iota(I32, shape, axis)


def split_two(values):
    head = values.astype(BF)
    return head, (values - head.astype(F32)).astype(BF)


def call(body, outs, ins, scratch=(), limit=16):
    return pl.pallas_call(
        body,
        out_shape=outs,
        in_specs=ins,
        out_specs=jax.tree.map(lambda _: VMEM, outs),
        scratch_shapes=list(scratch),
        compiler_params=pltpu.CompilerParams(vmem_limit_bytes=limit << 20),
    )


def send_kernel(hidden_ref, order_ref, cot_ref, out_ref):
    tokens, units = hidden_ref.shape
    pieces, per = out_ref.shape[:2]
    pick = order_ref[...] == iota((tokens, tokens), 0)
    rows = jnp.dot(
        jnp.where(pick, 1.0, 0.0).astype(BF), hidden_ref[...], preferred_element_type=F32
    )
    cot = jnp.sum(jnp.where(pick, cot_ref[...], 0.0), axis=1, keepdims=True)
    high = cot.astype(BF).astype(F32)
    rest = cot - high
    middle = rest.astype(BF).astype(F32)
    low = rest - middle
    lane = iota((tokens, LANES), 1)
    cols = jnp.where(lane == 0, high, jnp.where(lane == 1, middle, jnp.where(lane == 2, low, 0.0)))
    for p in range(pieces):
        at = slice(p * per, (p + 1) * per)
        out_ref[p] = jnp.concatenate([rows[at], cols[at]], axis=1).astype(BF)


def pool_kernel(dims, patch_ref, slot_ref, pooled_ref):
    y_n, h_n, x_n, l_n, c_n, two = dims
    tokens, patches = pooled_ref.shape[0], patch_ref.shape[0]
    shape = (tokens, patches)
    row = iota(shape, 0)
    near = x_n * l_n
    src = row // two % near * c_n + row // (near * two)
    match = (iota(shape, 1) // (patches // (near * c_n)) == src) & (slot_ref[...] == row % two)
    match = jnp.where(match, 1.0, 0.0)
    counts = jnp.sum(match, axis=1, keepdims=True)
    totals = jnp.dot(match.astype(BF), patch_ref[...], preferred_element_type=F32)
    pooled_ref[...] = (totals / counts).astype(BF)


def target_kernel(dims, pooled_ref, target_ref):
    y_n, h_n, x_n, l_n, c_n, two = dims
    near, per = x_n * l_n, c_n * two
    tokens = pooled_ref.shape[0]
    single = tokens // c_n
    row = iota((tokens, tokens), 0)
    wanted = (
        (row // two) % c_n * single + row // single * (near * two) + row // per % near * two + row % two
    )
    turn = jnp.where(wanted == iota((tokens, tokens), 1), 1.0, 0.0).astype(BF)
    step = 256
    for at in range(0, pooled_ref.shape[1], step):
        cut = slice(at, at + step)
        t = jnp.dot(turn, pooled_ref[:, cut], preferred_element_type=F32)
        target_ref[:, cut] = t.astype(BF)


def middle_kernel(
    dims, core_ref, high_ref, both_ref, target_ref, weight_ref, rest_ref, bias_ref, part_ref, back_ref,
    proj, grads, held, target, sems
):
    y_n, h_n, x_n, l_n, c_n, two = dims
    near, per = x_n * l_n, c_n * two
    tokens, units = both_ref.shape[0], both_ref.shape[1] - LANES
    first = weight_ref.shape[1]
    fetch_rest = pltpu.make_async_copy(rest_ref.at[:, pl.ds(first, LANES)], held, sems.at[1])
    fetch_rest.start()
    fetch = pltpu.make_async_copy(target_ref, target, sems.at[0])
    fetch.start()
    acts = both_ref[:, :units]
    width = rest_ref.shape[1]
    half = width // c_n
    single = tokens // c_n
    core = core_ref[0]
    step = 256
    s_pp = jnp.zeros((tokens, 1), F32)
    s_tt = jnp.zeros((tokens, 1), F32)
    s_pt = jnp.zeros((tokens, 1), F32)
    starts = list(range(0, first - step + 1, step))
    blocks = [(at, step) for at in starts] + [(at, LANES) for at in range(len(starts) * step, width, LANES)]
    for at, size in blocks:
        cut = slice(at, at + size)
        if at == first:
            fetch_rest.wait()
        block = held[...] if at == first else weight_ref[:, cut]
        p = jnp.dot(acts, block, preferred_element_type=F32) + bias_ref[:, cut]
        proj[:, cut] = p
        s_pp = s_pp + jnp.sum(p * p, axis=1, keepdims=True)
    fetch.wait()
    for at in range(0, width, step):
        cut = slice(at, at + step)
        t = target[:, cut].astype(F32)
        s_tt = s_tt + jnp.sum(t * t, axis=1, keepdims=True)
        s_pt = s_pt + jnp.sum(proj[:, cut] * t, axis=1, keepdims=True)
    inv_proj = lax.rsqrt(s_pp + 1e-06)
    inv_target = lax.rsqrt(s_tt + 1e-06)
    cosine = s_pt * inv_proj * inv_target
    terms = both_ref[:, units:].astype(F32)
    cot = (terms[:, 2:3] + terms[:, 1:2]) + terms[:, 0:1]
    scale_t = inv_proj * inv_target
    scale_p = cosine * inv_proj * inv_proj
    y_blocks = width // y_n // LANES
    tail_row = iota((TAIL, step), 0)
    main = part_ref.shape[1] - TAIL
    for at in range(0, width, step):
        g = cot * (target[:, at : at + step].astype(F32) * scale_t - scale_p * proj[:, at : at + step])
        g = g.astype(BF)
        inside = at % half
        grads[at // half, :, inside : inside + step] = g
        total = jnp.sum(g.astype(F32), axis=0, keepdims=True)
        high = total.astype(BF).astype(F32)
        tail = jnp.where(tail_row == 0, high, jnp.where(tail_row == 1, total - high, 0.0)).astype(BF)
        for k in range(step // LANES):
            block = at // LANES + k
            piece = block % y_blocks * y_n + block // y_blocks
            part_ref[piece, main:, :] = tail[:, k * LANES : (k + 1) * LANES]
    for y in range(y_n):
        for x in range(y_blocks, x_n):
            part_ref[x * y_n + y, main:, :] = jnp.zeros((TAIL, LANES), BF)
    lane = iota((tokens, LANES), 1)
    high, low = split_two(cosine)
    spot = iota((tokens, LANES), 0) % per == lane
    owner = iota((near, tokens), 1) - core * single
    chip = iota((near, tokens), 0)
    chip = chip % x_n * l_n + chip // x_n
    gather = jnp.where((owner >= 0) & (owner < single) & (owner // per == chip), 1.0, 0.0)
    gather = gather.astype(BF)
    back = jnp.zeros((near, LANES), F32)
    for term in (high, low):
        spread = jnp.where(spot, term.astype(F32), 0.0).astype(BF)
        back = back + jnp.dot(gather, spread, preferred_element_type=F32)
    back_ref[:near, :] = back
    back_ref[near:, :] = jnp.full((8, LANES), high_ref[0], I32).astype(F32)
    rows = units // y_n
    chunk = rows // h_n // x_n
    mine = grads[core]
    for y in range(y_n):
        product = lax.dot_general(
            acts[:, y * rows : (y + 1) * rows], mine, (((0,), (0,)), ((), ())), preferred_element_type=F32
        ).astype(BF)
        for h in range(h_n):
            for x in range(x_n):
                start = (h * x_n + x) * chunk
                for k in range(half // LANES):
                    to = (k * h_n + h) * chunk
                    part_ref[x * y_n + y, to : to + chunk, :] = product[
                        start : start + chunk, k * LANES : (k + 1) * LANES
                    ]


def plane_kernel(dims, part_ref, out_ref, spread):
    y_n, h_n, x_n, l_n, c_n, two = dims
    count, total_rows = part_ref.shape[0], part_ref.shape[1]
    main = total_rows - TAIL
    spread[...] = jnp.zeros_like(spread)
    group = out_ref.shape[0] // (h_n * l_n)
    lines = main // (h_n * l_n)

    def summed(start, size):
        total = part_ref[0, start : start + size, :].astype(F32)
        for p in range(1, count):
            total = total + part_ref[p, start : start + size, :].astype(F32)
        return total

    pair = lines // LINE_ROWS
    size = h_n * LINE_ROWS * l_n
    for k in range(pair):
        total = summed(k * size, size)
        for h in range(h_n):
            for r in range(LINE_ROWS):
                at = (h * LINE_ROWS + r) * l_n
                spread[pl.ds(h * group + k * LINE_ROWS + r, l_n, stride=h_n * group), :] = total[at : at + l_n]
    tail = summed(main, TAIL)
    bias = tail[0:1] + tail[1:2]
    high = bias.astype(BF).astype(F32)
    for r, value in enumerate((high, bias - high)):
        full = jnp.broadcast_to(value, (h_n * l_n, LANES))
        spread[pl.ds(lines + r, h_n * l_n, stride=group), :] = full
    out_ref[...] = spread[...].astype(BF)


def line_kernel(lines, part_ref, back_ref, out_ref):
    total = part_ref[0].astype(F32)
    for p in range(1, part_ref.shape[0]):
        total = total + part_ref[p].astype(F32)
    group = total.shape[0]
    row = iota((group, LANES), 0)
    bias = total[lines : lines + 1] + total[lines + 1 : lines + 2]
    high = bias.astype(BF).astype(F32)
    total = jnp.where(row == lines, high, jnp.where(row == lines + 1, bias - high, total))
    for p in range(out_ref.shape[0]):
        value = back_ref[p : p + 1, :]
        head = value.astype(BF).astype(F32)
        tile = jnp.where(row == group - 2, head, jnp.where(row == group - 1, value - head, total))
        out_ref[p] = tile.astype(BF)


def unpack_kernel(
    dims, back_ref, own_ref, both_ref, order_ref, cos_ref, weight_ref, bias_ref, wide, narrow
):
    y_n, h_n, x_n, l_n, c_n, two = dims
    near, per = x_n * l_n, c_n * two
    group = own_ref.shape[0] // near
    wide[...] = both_ref[...].astype(F32)
    narrow[...] = own_ref[...].astype(F32)
    half = weight_ref.shape[1] // c_n
    pairs = half // LANES
    lines = pairs * LINE_ROWS
    for c in range(c_n):
        for x in range(x_n):
            for k in range(pairs):
                for r in range(LINE_ROWS):
                    start = (c * near + x) * group + k * LINE_ROWS + r
                    to = (x * LINE_ROWS + r) * l_n
                    at = c * half + k * LANES
                    weight_ref[to : to + l_n, at : at + LANES] = wide[pl.ds(start, l_n, stride=x_n * group), :]
    cosines = narrow[pl.ds(group - 2, near, stride=group), :] + narrow[pl.ds(group - 1, near, stride=group), :]
    order = order_ref[...]
    tokens = order.shape[1]
    chip = iota((near, tokens), 0)
    base = (chip % x_n * l_n + chip // x_n) * per
    total = jnp.zeros((near, tokens), F32)
    for i in range(per):
        total = total + jnp.where(order == base + i, cosines[:, i : i + 1], 0.0)
    cos_ref[...] = jnp.sum(total, axis=0, keepdims=True)
    cols = bias_ref.shape[1]
    blocks = cols * h_n // LANES
    offset = back_ref[near:, :cols].astype(I32)[0:1] * cols
    out = jnp.zeros((8, cols), F32)
    for b in range(blocks):
        start = b * group + lines
        pick = iota((LANES, cols), 0) + b * LANES == iota((LANES, cols), 1) + offset
        pick = jnp.where(pick, 1.0, 0.0).astype(BF)
        for r in range(2):
            term = jnp.broadcast_to(narrow[start + r : start + r + 1, :], (8, LANES)).astype(BF)
            out = out + jnp.dot(term, pick, preferred_element_type=F32)
    bias_ref[...] = out[0:1]


def local(hidden, weight, bias, patches, slots, order, cotangent):
    y_n, h_n, x_n, l_n, c_n = (lax.axis_size(a) for a in ("y", "h", "x", "l", "c"))
    patches = patches[0]
    tokens, units = hidden.shape[1:]
    width = weight.shape[1]
    near = x_n * l_n
    per = tokens // near
    shards = near * c_n
    two = tokens // shards
    half = width // c_n
    dims = (y_n, h_n, x_n, l_n, c_n, two)
    shape = jax.ShapeDtypeStruct
    core = lax.axis_index("c").astype(I32)[None]
    high = lax.axis_index("h").astype(I32)[None]

    sent = call(send_kernel, shape((near, per, units + LANES), BF), [VMEM] * 3, limit=60)(
        hidden[0], order, cotangent
    )
    moved = lax.all_to_all(sent, ("x", "l"), 0, 0, tiled=True)
    pooled = call(
        functools.partial(pool_kernel, dims), shape((tokens, width), BF), [VMEM] * 2, limit=60
    )(patches, slots)
    pooled = lax.all_gather(pooled, "c", axis=0, tiled=True)
    target = call(
        functools.partial(target_kernel, dims), shape((c_n * tokens, width), BF), [VMEM], limit=60
    )(pooled)
    target = pltpu.with_memory_space_constraint(target, pltpu.HBM)

    both = lax.all_gather(moved.reshape(tokens, units + LANES), "c", axis=0, tiled=True)
    rows = units // (y_n * x_n)
    lines = half // LANES * LINE_ROWS
    part, back = call(
        functools.partial(middle_kernel, dims),
        (
            shape((y_n * x_n, rows * half // LANES + TAIL, LANES), BF),
            shape((near + 8, LANES), F32),
        ),
        [SMEM] * 2 + [VMEM, HBM, VMEM, HBM, VMEM],
        [
            pltpu.VMEM((c_n * tokens, width), F32),
            pltpu.VMEM((c_n, c_n * tokens, half), BF),
            pltpu.VMEM((units, LANES), BF),
            pltpu.VMEM((c_n * tokens, width), BF),
            pltpu.SemaphoreType.DMA((2,)),
        ],
    )(core, high, both, target, weight[:, : width - LANES], pltpu.with_memory_space_constraint(weight, pltpu.HBM), bias[None, :])

    part = lax.all_to_all(part, ("x", "y"), 0, 0, tiled=True)
    spots = h_n * l_n
    part = call(
        functools.partial(plane_kernel, dims),
        shape((spots * TAIL, LANES), BF),
        [VMEM],
        [pltpu.VMEM((spots * TAIL, LANES), F32)],
    )(part)
    part, back = lax.optimization_barrier((part, back))
    part = lax.all_to_all(part.reshape(spots, TAIL, LANES), ("l", "h"), 0, 0, tiled=True)
    part = call(functools.partial(line_kernel, lines), shape((near, TAIL, LANES), BF), [VMEM] * 2)(part, back)
    part = lax.all_to_all(part, ("l", "x"), 0, 0, tiled=True).reshape(near * TAIL, LANES)
    wide = lax.all_gather(part, "c", axis=0, tiled=True)
    cos_sim, weight_grad, bias_grad = call(
        functools.partial(unpack_kernel, dims),
        (
            shape((1, tokens), F32),
            shape((units // (y_n * h_n), width), F32),
            shape((1, width // (y_n * h_n)), F32),
        ),
        [VMEM] * 4,
        [pltpu.VMEM((c_n * near * TAIL, LANES), F32), pltpu.VMEM((near * TAIL, LANES), F32)],
    )(back, part, wide, order)
    return cos_sim, weight_grad, bias_grad[0]


def solution(mesh, sizes=(4, 4, 4, 8, 2)):
    fine = Mesh(mesh.devices.reshape(sizes), ("y", "h", "x", "l", "c"))
    clip, seq = ("y", "h"), ("x", "l", "c")
    placed = (
        P(clip, seq, None),
        P(),
        P(),
        P(clip, seq, None),
        P(clip, seq),
        P(clip, seq),
        P(clip, seq),
    )
    return jax.shard_map(
        local,
        mesh=fine,
        in_specs=placed,
        out_specs=(P(clip, seq), P(clip, None), P(clip)),
        check_vma=False,
    )
```

```python
import functools

import jax
import jax.numpy as jnp
from jax import lax
from jax.experimental import pallas as pl
from jax.experimental.pallas import tpu as pltpu
from jax.sharding import Mesh, PartitionSpec as P

BF = jnp.bfloat16
F32 = jnp.float32
I32 = jnp.int32
LANES = 128
TAIL = 16
LINE_ROWS = 2
VMEM = pl.BlockSpec(memory_space=pltpu.VMEM)
SMEM = pl.BlockSpec(memory_space=pltpu.SMEM)
HBM = pl.BlockSpec(memory_space=pltpu.HBM)


def iota(shape, axis):
    return lax.broadcasted_iota(I32, shape, axis)


def split_two(values):
    head = values.astype(BF)
    return head, (values - head.astype(F32)).astype(BF)


def call(body, outs, ins, scratch=(), limit=16):
    return pl.pallas_call(
        body,
        out_shape=outs,
        in_specs=ins,
        out_specs=jax.tree.map(lambda _: VMEM, outs),
        scratch_shapes=list(scratch),
        compiler_params=pltpu.CompilerParams(vmem_limit_bytes=limit << 20),
    )


def send_kernel(hidden_ref, order_ref, cot_ref, out_ref):
    tokens, units = hidden_ref.shape
    pieces, per = out_ref.shape[:2]
    pick = order_ref[...] == iota((tokens, tokens), 0)
    rows = jnp.dot(
        jnp.where(pick, 1.0, 0.0).astype(BF), hidden_ref[...], preferred_element_type=F32
    )
    cot = jnp.sum(jnp.where(pick, cot_ref[...], 0.0), axis=1, keepdims=True)
    high = cot.astype(BF).astype(F32)
    rest = cot - high
    middle = rest.astype(BF).astype(F32)
    low = rest - middle
    lane = iota((tokens, LANES), 1)
    cols = jnp.where(lane == 0, high, jnp.where(lane == 1, middle, jnp.where(lane == 2, low, 0.0)))
    for p in range(pieces):
        at = slice(p * per, (p + 1) * per)
        out_ref[p] = jnp.concatenate([rows[at], cols[at]], axis=1).astype(BF)


def pool_kernel(dims, patch_ref, slot_ref, pooled_ref):
    y_n, h_n, x_n, l_n, c_n, two = dims
    tokens, patches = pooled_ref.shape[0], patch_ref.shape[0]
    shape = (tokens, patches)
    row = iota(shape, 0)
    near = x_n * l_n
    src = row // two % near * c_n + row // (near * two)
    match = (iota(shape, 1) // (patches // (near * c_n)) == src) & (slot_ref[...] == row % two)
    match = jnp.where(match, 1.0, 0.0)
    counts = jnp.sum(match, axis=1, keepdims=True)
    totals = jnp.dot(match.astype(BF), patch_ref[...], preferred_element_type=F32)
    pooled_ref[...] = (totals / counts).astype(BF)


def middle_kernel(
    dims, core_ref, high_ref, both_ref, pooled_ref, weight_ref, rest_ref, bias_ref, part_ref, back_ref,
    proj, target, grads, held, pooled, sems
):
    y_n, h_n, x_n, l_n, c_n, two = dims
    near, per = x_n * l_n, c_n * two
    tokens, units = both_ref.shape[0], both_ref.shape[1] - LANES
    first = weight_ref.shape[1]
    fetch_rest = pltpu.make_async_copy(rest_ref.at[:, pl.ds(first, LANES)], held, sems.at[1])
    fetch_rest.start()
    fetch = pltpu.make_async_copy(pooled_ref, pooled, sems.at[0])
    fetch.start()
    acts = both_ref[:, :units]
    width = rest_ref.shape[1]
    half = width // c_n
    single = tokens // c_n
    core = core_ref[0]
    row = iota((tokens, tokens), 0)
    wanted = (
        (row // two) % c_n * single + row // single * (near * two) + row // per % near * two + row % two
    )
    turn = jnp.where(wanted == iota((tokens, tokens), 1), 1.0, 0.0).astype(BF)
    step = 256
    s_pp = jnp.zeros((tokens, 1), F32)
    s_tt = jnp.zeros((tokens, 1), F32)
    s_pt = jnp.zeros((tokens, 1), F32)
    starts = list(range(0, first - step + 1, step))
    blocks = [(at, step) for at in starts] + [(at, LANES) for at in range(len(starts) * step, width, LANES)]
    for at, size in blocks:
        cut = slice(at, at + size)
        if at == first:
            fetch_rest.wait()
        block = held[...] if at == first else weight_ref[:, cut]
        p = jnp.dot(acts, block, preferred_element_type=F32) + bias_ref[:, cut]
        proj[:, cut] = p
        s_pp = s_pp + jnp.sum(p * p, axis=1, keepdims=True)
    fetch.wait()
    for at in range(0, width, step):
        cut = slice(at, at + step)
        t = jnp.dot(turn, pooled[:, cut], preferred_element_type=F32)
        target[:, cut] = t
        s_tt = s_tt + jnp.sum(t * t, axis=1, keepdims=True)
        s_pt = s_pt + jnp.sum(proj[:, cut] * t, axis=1, keepdims=True)
    inv_proj = lax.rsqrt(s_pp + 1e-06)
    inv_target = lax.rsqrt(s_tt + 1e-06)
    cosine = s_pt * inv_proj * inv_target
    terms = both_ref[:, units:].astype(F32)
    cot = (terms[:, 2:3] + terms[:, 1:2]) + terms[:, 0:1]
    scale_t = inv_proj * inv_target
    scale_p = cosine * inv_proj * inv_proj
    y_blocks = width // y_n // LANES
    tail_row = iota((TAIL, step), 0)
    main = part_ref.shape[1] - TAIL
    for at in range(0, width, step):
        g = cot * (target[:, at : at + step] * scale_t - scale_p * proj[:, at : at + step])
        g = g.astype(BF)
        inside = at % half
        grads[at // half, :, inside : inside + step] = g
        total = jnp.sum(g.astype(F32), axis=0, keepdims=True)
        high = total.astype(BF).astype(F32)
        tail = jnp.where(tail_row == 0, high, jnp.where(tail_row == 1, total - high, 0.0)).astype(BF)
        for k in range(step // LANES):
            block = at // LANES + k
            piece = block // y_blocks * x_n + block % y_blocks
            part_ref[piece, main:, :] = tail[:, k * LANES : (k + 1) * LANES]
    for y in range(y_n):
        for x in range(y_blocks, x_n):
            part_ref[y * x_n + x, main:, :] = jnp.zeros((TAIL, LANES), BF)
    lane = iota((tokens, LANES), 1)
    high, low = split_two(cosine)
    spot = iota((tokens, LANES), 0) % per == lane
    owner = iota((near, tokens), 1) - core * single
    gather = jnp.where((owner >= 0) & (owner < single) & (owner // per == iota((near, tokens), 0)), 1.0, 0.0)
    gather = gather.astype(BF)
    back = jnp.zeros((near, LANES), F32)
    for term in (high, low):
        spread = jnp.where(spot, term.astype(F32), 0.0).astype(BF)
        back = back + jnp.dot(gather, spread, preferred_element_type=F32)
    back_ref[:near, :] = back
    back_ref[near:, :] = jnp.full((8, LANES), high_ref[0], I32).astype(F32)
    rows = units // y_n
    chunk = rows // h_n // x_n
    mine = grads[core]
    for y in range(y_n):
        product = lax.dot_general(
            acts[:, y * rows : (y + 1) * rows], mine, (((0,), (0,)), ((), ())), preferred_element_type=F32
        ).astype(BF)
        for h in range(h_n):
            for x in range(x_n):
                start = (h * x_n + x) * chunk
                for k in range(half // LANES):
                    to = (k * h_n + h) * chunk
                    part_ref[y * x_n + x, to : to + chunk, :] = product[
                        start : start + chunk, k * LANES : (k + 1) * LANES
                    ]


def plane_kernel(dims, part_ref, out_ref, spread):
    y_n, h_n, x_n, l_n, c_n, two = dims
    count, total_rows = part_ref.shape[0], part_ref.shape[1]
    main = total_rows - TAIL
    spread[...] = jnp.zeros_like(spread)
    group = out_ref.shape[0] // (h_n * l_n)
    lines = main // (h_n * l_n)

    def summed(start, size):
        total = part_ref[0, start : start + size, :].astype(F32)
        for p in range(1, count):
            total = total + part_ref[p, start : start + size, :].astype(F32)
        return total

    pair = lines // LINE_ROWS
    size = h_n * LINE_ROWS * l_n
    for k in range(pair):
        total = summed(k * size, size)
        for h in range(h_n):
            for r in range(LINE_ROWS):
                at = (h * LINE_ROWS + r) * l_n
                spread[pl.ds(h * l_n * group + k * LINE_ROWS + r, l_n, stride=group), :] = total[at : at + l_n]
    tail = summed(main, TAIL)
    bias = tail[0:1] + tail[1:2]
    high = bias.astype(BF).astype(F32)
    for r, value in enumerate((high, bias - high)):
        full = jnp.broadcast_to(value, (h_n * l_n, LANES))
        spread[pl.ds(lines + r, h_n * l_n, stride=group), :] = full
    out_ref[...] = spread[...].astype(BF)


def line_kernel(lines, part_ref, back_ref, out_ref):
    total = part_ref[0].astype(F32)
    for p in range(1, part_ref.shape[0]):
        total = total + part_ref[p].astype(F32)
    group = total.shape[0]
    row = iota((group, LANES), 0)
    bias = total[lines : lines + 1] + total[lines + 1 : lines + 2]
    high = bias.astype(BF).astype(F32)
    total = jnp.where(row == lines, high, jnp.where(row == lines + 1, bias - high, total))
    for p in range(out_ref.shape[0]):
        value = back_ref[p : p + 1, :]
        head = value.astype(BF).astype(F32)
        tile = jnp.where(row == group - 2, head, jnp.where(row == group - 1, value - head, total))
        out_ref[p] = tile.astype(BF)


def unpack_kernel(
    dims, back_ref, own_ref, both_ref, order_ref, cos_ref, weight_ref, bias_ref, wide, narrow
):
    y_n, h_n, x_n, l_n, c_n, two = dims
    near, per = x_n * l_n, c_n * two
    group = own_ref.shape[0] // near
    wide[...] = both_ref[...].astype(F32)
    narrow[...] = own_ref[...].astype(F32)
    half = weight_ref.shape[1] // c_n
    pairs = half // LANES
    lines = pairs * LINE_ROWS
    for c in range(c_n):
        for x in range(x_n):
            for k in range(pairs):
                for r in range(LINE_ROWS):
                    start = (c * near + x * l_n) * group + k * LINE_ROWS + r
                    to = (x * LINE_ROWS + r) * l_n
                    at = c * half + k * LANES
                    weight_ref[to : to + l_n, at : at + LANES] = wide[pl.ds(start, l_n, stride=group), :]
    cosines = narrow[pl.ds(group - 2, near, stride=group), :] + narrow[pl.ds(group - 1, near, stride=group), :]
    order = order_ref[...]
    tokens = order.shape[1]
    base = iota((near, tokens), 0) * per
    total = jnp.zeros((near, tokens), F32)
    for i in range(per):
        total = total + jnp.where(order == base + i, cosines[:, i : i + 1], 0.0)
    cos_ref[...] = jnp.sum(total, axis=0, keepdims=True)
    cols = bias_ref.shape[1]
    blocks = cols * h_n // LANES
    offset = back_ref[near:, :cols].astype(I32)[0:1] * cols
    out = jnp.zeros((8, cols), F32)
    for b in range(blocks):
        start = b * l_n * group + lines
        pick = iota((LANES, cols), 0) + b * LANES == iota((LANES, cols), 1) + offset
        pick = jnp.where(pick, 1.0, 0.0).astype(BF)
        for r in range(2):
            term = jnp.broadcast_to(narrow[start + r : start + r + 1, :], (8, LANES)).astype(BF)
            out = out + jnp.dot(term, pick, preferred_element_type=F32)
    bias_ref[...] = out[0:1]


def local(hidden, weight, bias, patches, slots, order, cotangent):
    y_n, h_n, x_n, l_n, c_n = (lax.axis_size(a) for a in ("y", "h", "x", "l", "c"))
    patches = patches[0]
    tokens, units = hidden.shape[1:]
    width = weight.shape[1]
    near = x_n * l_n
    per = tokens // near
    shards = near * c_n
    two = tokens // shards
    half = width // c_n
    dims = (y_n, h_n, x_n, l_n, c_n, two)
    shape = jax.ShapeDtypeStruct
    core = lax.axis_index("c").astype(I32)[None]
    high = lax.axis_index("h").astype(I32)[None]

    sent = call(send_kernel, shape((near, per, units + LANES), BF), [VMEM] * 3, limit=60)(
        hidden[0], order, cotangent
    )
    moved = lax.all_to_all(sent, ("x", "l"), 0, 0, tiled=True)
    pooled = call(
        functools.partial(pool_kernel, dims), shape((tokens, width), BF), [VMEM] * 2, limit=60
    )(patches, slots)
    pooled = lax.all_gather(pooled, "c", axis=0, tiled=True)
    pooled = pltpu.with_memory_space_constraint(pooled, pltpu.HBM)

    both = lax.all_gather(moved.reshape(tokens, units + LANES), "c", axis=0, tiled=True)
    rows = units // (y_n * x_n)
    lines = half // LANES * LINE_ROWS
    part, back = call(
        functools.partial(middle_kernel, dims),
        (
            shape((y_n * x_n, rows * half // LANES + TAIL, LANES), BF),
            shape((near + 8, LANES), F32),
        ),
        [SMEM] * 2 + [VMEM, HBM, VMEM, HBM, VMEM],
        [
            pltpu.VMEM((c_n * tokens, width), F32),
            pltpu.VMEM((c_n * tokens, width), F32),
            pltpu.VMEM((c_n, c_n * tokens, half), BF),
            pltpu.VMEM((units, LANES), BF),
            pltpu.VMEM((c_n * tokens, width), BF),
            pltpu.SemaphoreType.DMA((2,)),
        ],
    )(core, high, both, pooled, weight[:, : width - LANES], pltpu.with_memory_space_constraint(weight, pltpu.HBM), bias[None, :])

    part = lax.all_to_all(part, ("y", "x"), 0, 0, tiled=True)
    spots = h_n * l_n
    part = call(
        functools.partial(plane_kernel, dims),
        shape((spots * TAIL, LANES), BF),
        [VMEM],
        [pltpu.VMEM((spots * TAIL, LANES), F32)],
    )(part)
    part, back = lax.optimization_barrier((part, back))
    part = lax.all_to_all(part.reshape(spots, TAIL, LANES), ("h", "l"), 0, 0, tiled=True)
    part = call(functools.partial(line_kernel, lines), shape((near, TAIL, LANES), BF), [VMEM] * 2)(part, back)
    part = lax.all_to_all(part, ("x", "l"), 0, 0, tiled=True).reshape(near * TAIL, LANES)
    wide = lax.all_gather(part, "c", axis=0, tiled=True)
    cos_sim, weight_grad, bias_grad = call(
        functools.partial(unpack_kernel, dims),
        (
            shape((1, tokens), F32),
            shape((units // (y_n * h_n), width), F32),
            shape((1, width // (y_n * h_n)), F32),
        ),
        [VMEM] * 4,
        [pltpu.VMEM((c_n * near * TAIL, LANES), F32), pltpu.VMEM((near * TAIL, LANES), F32)],
    )(back, part, wide, order)
    return cos_sim, weight_grad, bias_grad[0]


def solution(mesh, sizes=(4, 4, 4, 8, 2)):
    fine = Mesh(mesh.devices.reshape(sizes), ("y", "h", "x", "l", "c"))
    clip, seq = ("y", "h"), ("x", "l", "c")
    placed = (
        P(clip, seq, None),
        P(),
        P(),
        P(clip, seq, None),
        P(clip, seq),
        P(clip, seq),
        P(clip, seq),
    )
    return jax.shard_map(
        local,
        mesh=fine,
        in_specs=placed,
        out_specs=(P(clip, seq), P(clip, None), P(clip)),
        check_vma=False,
    )
```

```python
import functools

import jax
import jax.numpy as jnp
from jax import lax
from jax.experimental import pallas as pl
from jax.experimental.pallas import tpu as pltpu
from jax.sharding import Mesh, PartitionSpec as P

BF = jnp.bfloat16
F32 = jnp.float32
I32 = jnp.int32
LANES = 128
TAIL = 16
LINE_ROWS = 2
VMEM = pl.BlockSpec(memory_space=pltpu.VMEM)
SMEM = pl.BlockSpec(memory_space=pltpu.SMEM)
HBM = pl.BlockSpec(memory_space=pltpu.HBM)


def iota(shape, axis):
    return lax.broadcasted_iota(I32, shape, axis)


def split_two(values):
    head = values.astype(BF)
    return head, (values - head.astype(F32)).astype(BF)


def call(body, outs, ins, scratch=(), limit=16):
    return pl.pallas_call(
        body,
        out_shape=outs,
        in_specs=ins,
        out_specs=jax.tree.map(lambda _: VMEM, outs),
        scratch_shapes=list(scratch),
        compiler_params=pltpu.CompilerParams(vmem_limit_bytes=limit << 20),
    )


def send_kernel(hidden_ref, order_ref, cot_ref, out_ref):
    tokens, units = hidden_ref.shape
    pieces, per = out_ref.shape[:2]
    pick = order_ref[...] == iota((tokens, tokens), 0)
    rows = jnp.dot(
        jnp.where(pick, 1.0, 0.0).astype(BF), hidden_ref[...], preferred_element_type=F32
    )
    cot = jnp.sum(jnp.where(pick, cot_ref[...], 0.0), axis=1, keepdims=True)
    high = cot.astype(BF).astype(F32)
    rest = cot - high
    middle = rest.astype(BF).astype(F32)
    low = rest - middle
    lane = iota((tokens, LANES), 1)
    cols = jnp.where(lane == 0, high, jnp.where(lane == 1, middle, jnp.where(lane == 2, low, 0.0)))
    for p in range(pieces):
        at = slice(p * per, (p + 1) * per)
        out_ref[p] = jnp.concatenate([rows[at], cols[at]], axis=1).astype(BF)


def pool_kernel(dims, patch_ref, slot_ref, pooled_ref):
    y_n, h_n, x_n, l_n, c_n, two = dims
    tokens, patches = pooled_ref.shape[0], patch_ref.shape[0]
    shape = (tokens, patches)
    row = iota(shape, 0)
    near = x_n * l_n
    src = row // two % near * c_n + row // (near * two)
    match = (iota(shape, 1) // (patches // (near * c_n)) == src) & (slot_ref[...] == row % two)
    match = jnp.where(match, 1.0, 0.0)
    counts = jnp.sum(match, axis=1, keepdims=True)
    totals = jnp.dot(match.astype(BF), patch_ref[...], preferred_element_type=F32)
    pooled_ref[...] = (totals / counts).astype(BF)


def target_kernel(dims, pooled_ref, target_ref):
    y_n, h_n, x_n, l_n, c_n, two = dims
    near, per = x_n * l_n, c_n * two
    tokens = pooled_ref.shape[0]
    single = tokens // c_n
    row = iota((tokens, tokens), 0)
    wanted = (
        (row // two) % c_n * single + row // single * (near * two) + row // per % near * two + row % two
    )
    turn = jnp.where(wanted == iota((tokens, tokens), 1), 1.0, 0.0).astype(BF)
    step = 256
    for at in range(0, pooled_ref.shape[1], step):
        cut = slice(at, at + step)
        t = jnp.dot(turn, pooled_ref[:, cut], preferred_element_type=F32)
        target_ref[:, cut] = t.astype(BF)


def middle_kernel(
    dims, core_ref, high_ref, both_ref, target_ref, weight_ref, rest_ref, bias_ref, part_ref, back_ref,
    proj, grads, held, target, sems
):
    y_n, h_n, x_n, l_n, c_n, two = dims
    near, per = x_n * l_n, c_n * two
    tokens, units = both_ref.shape[0], both_ref.shape[1] - LANES
    first = weight_ref.shape[1]
    fetch_rest = pltpu.make_async_copy(rest_ref.at[:, pl.ds(first, LANES)], held, sems.at[1])
    fetch_rest.start()
    fetch = pltpu.make_async_copy(target_ref, target, sems.at[0])
    fetch.start()
    acts = both_ref[:, :units]
    width = rest_ref.shape[1]
    half = width // c_n
    single = tokens // c_n
    core = core_ref[0]
    step = 256
    s_pp = jnp.zeros((tokens, 1), F32)
    s_tt = jnp.zeros((tokens, 1), F32)
    s_pt = jnp.zeros((tokens, 1), F32)
    starts = list(range(0, first - step + 1, step))
    blocks = [(at, step) for at in starts] + [(at, LANES) for at in range(len(starts) * step, width, LANES)]
    for at, size in blocks:
        cut = slice(at, at + size)
        if at == first:
            fetch_rest.wait()
        block = held[...] if at == first else weight_ref[:, cut]
        p = jnp.dot(acts, block, preferred_element_type=F32) + bias_ref[:, cut]
        proj[:, cut] = p
        s_pp = s_pp + jnp.sum(p * p, axis=1, keepdims=True)
    fetch.wait()
    for at in range(0, width, step):
        cut = slice(at, at + step)
        t = target[:, cut].astype(F32)
        s_tt = s_tt + jnp.sum(t * t, axis=1, keepdims=True)
        s_pt = s_pt + jnp.sum(proj[:, cut] * t, axis=1, keepdims=True)
    inv_proj = lax.rsqrt(s_pp + 1e-06)
    inv_target = lax.rsqrt(s_tt + 1e-06)
    cosine = s_pt * inv_proj * inv_target
    terms = both_ref[:, units:].astype(F32)
    cot = (terms[:, 2:3] + terms[:, 1:2]) + terms[:, 0:1]
    scale_t = inv_proj * inv_target
    scale_p = cosine * inv_proj * inv_proj
    y_blocks = width // y_n // LANES
    tail_row = iota((TAIL, step), 0)
    main = part_ref.shape[1] - TAIL
    for at in range(0, width, step):
        g = cot * (target[:, at : at + step].astype(F32) * scale_t - scale_p * proj[:, at : at + step])
        g = g.astype(BF)
        inside = at % half
        grads[at // half, :, inside : inside + step] = g
        total = jnp.sum(g.astype(F32), axis=0, keepdims=True)
        high = total.astype(BF).astype(F32)
        tail = jnp.where(tail_row == 0, high, jnp.where(tail_row == 1, total - high, 0.0)).astype(BF)
        for k in range(step // LANES):
            block = at // LANES + k
            piece = block // y_blocks * x_n + block % y_blocks
            part_ref[piece, main:, :] = tail[:, k * LANES : (k + 1) * LANES]
    for y in range(y_n):
        for x in range(y_blocks, x_n):
            part_ref[y * x_n + x, main:, :] = jnp.zeros((TAIL, LANES), BF)
    lane = iota((tokens, LANES), 1)
    high, low = split_two(cosine)
    spot = iota((tokens, LANES), 0) % per == lane
    owner = iota((near, tokens), 1) - core * single
    gather = jnp.where((owner >= 0) & (owner < single) & (owner // per == iota((near, tokens), 0)), 1.0, 0.0)
    gather = gather.astype(BF)
    back = jnp.zeros((near, LANES), F32)
    for term in (high, low):
        spread = jnp.where(spot, term.astype(F32), 0.0).astype(BF)
        back = back + jnp.dot(gather, spread, preferred_element_type=F32)
    back_ref[:near, :] = back
    back_ref[near:, :] = jnp.full((8, LANES), high_ref[0], I32).astype(F32)
    rows = units // y_n
    chunk = rows // h_n // x_n
    mine = grads[core]
    for y in range(y_n):
        product = lax.dot_general(
            acts[:, y * rows : (y + 1) * rows], mine, (((0,), (0,)), ((), ())), preferred_element_type=F32
        ).astype(BF)
        for h in range(h_n):
            for x in range(x_n):
                start = (h * x_n + x) * chunk
                for k in range(half // LANES):
                    to = (k * h_n + h) * chunk
                    part_ref[y * x_n + x, to : to + chunk, :] = product[
                        start : start + chunk, k * LANES : (k + 1) * LANES
                    ]


def plane_kernel(dims, part_ref, out_ref, spread):
    y_n, h_n, x_n, l_n, c_n, two = dims
    count, total_rows = part_ref.shape[0], part_ref.shape[1]
    main = total_rows - TAIL
    spread[...] = jnp.zeros_like(spread)
    group = out_ref.shape[0] // (h_n * l_n)
    lines = main // (h_n * l_n)

    def summed(start, size):
        total = part_ref[0, start : start + size, :].astype(F32)
        for p in range(1, count):
            total = total + part_ref[p, start : start + size, :].astype(F32)
        return total

    pair = lines // LINE_ROWS
    size = h_n * LINE_ROWS * l_n
    for k in range(pair):
        total = summed(k * size, size)
        for h in range(h_n):
            for r in range(LINE_ROWS):
                at = (h * LINE_ROWS + r) * l_n
                spread[pl.ds(h * l_n * group + k * LINE_ROWS + r, l_n, stride=group), :] = total[at : at + l_n]
    tail = summed(main, TAIL)
    bias = tail[0:1] + tail[1:2]
    high = bias.astype(BF).astype(F32)
    for r, value in enumerate((high, bias - high)):
        full = jnp.broadcast_to(value, (h_n * l_n, LANES))
        spread[pl.ds(lines + r, h_n * l_n, stride=group), :] = full
    out_ref[...] = spread[...].astype(BF)


def line_kernel(lines, part_ref, back_ref, out_ref):
    total = part_ref[0].astype(F32)
    for p in range(1, part_ref.shape[0]):
        total = total + part_ref[p].astype(F32)
    group = total.shape[0]
    row = iota((group, LANES), 0)
    bias = total[lines : lines + 1] + total[lines + 1 : lines + 2]
    high = bias.astype(BF).astype(F32)
    total = jnp.where(row == lines, high, jnp.where(row == lines + 1, bias - high, total))
    for p in range(out_ref.shape[0]):
        value = back_ref[p : p + 1, :]
        head = value.astype(BF).astype(F32)
        tile = jnp.where(row == group - 2, head, jnp.where(row == group - 1, value - head, total))
        out_ref[p] = tile.astype(BF)


def unpack_kernel(
    dims, back_ref, own_ref, both_ref, order_ref, cos_ref, weight_ref, bias_ref, wide, narrow
):
    y_n, h_n, x_n, l_n, c_n, two = dims
    near, per = x_n * l_n, c_n * two
    group = own_ref.shape[0] // near
    wide[...] = both_ref[...].astype(F32)
    narrow[...] = own_ref[...].astype(F32)
    half = weight_ref.shape[1] // c_n
    pairs = half // LANES
    lines = pairs * LINE_ROWS
    for c in range(c_n):
        for x in range(x_n):
            for k in range(pairs):
                for r in range(LINE_ROWS):
                    start = (c * near + x * l_n) * group + k * LINE_ROWS + r
                    to = (x * LINE_ROWS + r) * l_n
                    at = c * half + k * LANES
                    weight_ref[to : to + l_n, at : at + LANES] = wide[pl.ds(start, l_n, stride=group), :]
    cosines = narrow[pl.ds(group - 2, near, stride=group), :] + narrow[pl.ds(group - 1, near, stride=group), :]
    order = order_ref[...]
    tokens = order.shape[1]
    base = iota((near, tokens), 0) * per
    total = jnp.zeros((near, tokens), F32)
    for i in range(per):
        total = total + jnp.where(order == base + i, cosines[:, i : i + 1], 0.0)
    cos_ref[...] = jnp.sum(total, axis=0, keepdims=True)
    cols = bias_ref.shape[1]
    blocks = cols * h_n // LANES
    offset = back_ref[near:, :cols].astype(I32)[0:1] * cols
    out = jnp.zeros((8, cols), F32)
    for b in range(blocks):
        start = b * l_n * group + lines
        pick = iota((LANES, cols), 0) + b * LANES == iota((LANES, cols), 1) + offset
        pick = jnp.where(pick, 1.0, 0.0).astype(BF)
        for r in range(2):
            term = jnp.broadcast_to(narrow[start + r : start + r + 1, :], (8, LANES)).astype(BF)
            out = out + jnp.dot(term, pick, preferred_element_type=F32)
    bias_ref[...] = out[0:1]


def local(hidden, weight, bias, patches, slots, order, cotangent):
    y_n, h_n, x_n, l_n, c_n = (lax.axis_size(a) for a in ("y", "h", "x", "l", "c"))
    patches = patches[0]
    tokens, units = hidden.shape[1:]
    width = weight.shape[1]
    near = x_n * l_n
    per = tokens // near
    shards = near * c_n
    two = tokens // shards
    half = width // c_n
    dims = (y_n, h_n, x_n, l_n, c_n, two)
    shape = jax.ShapeDtypeStruct
    core = lax.axis_index("c").astype(I32)[None]
    high = lax.axis_index("h").astype(I32)[None]

    sent = call(send_kernel, shape((near, per, units + LANES), BF), [VMEM] * 3, limit=60)(
        hidden[0], order, cotangent
    )
    moved = lax.all_to_all(sent, ("x", "l"), 0, 0, tiled=True)
    pooled = call(
        functools.partial(pool_kernel, dims), shape((tokens, width), BF), [VMEM] * 2, limit=60
    )(patches, slots)
    pooled = lax.all_gather(pooled, "c", axis=0, tiled=True)
    target = call(
        functools.partial(target_kernel, dims), shape((c_n * tokens, width), BF), [VMEM], limit=60
    )(pooled)
    target = pltpu.with_memory_space_constraint(target, pltpu.HBM)

    both = lax.all_gather(moved.reshape(tokens, units + LANES), "c", axis=0, tiled=True)
    rows = units // (y_n * x_n)
    lines = half // LANES * LINE_ROWS
    part, back = call(
        functools.partial(middle_kernel, dims),
        (
            shape((y_n * x_n, rows * half // LANES + TAIL, LANES), BF),
            shape((near + 8, LANES), F32),
        ),
        [SMEM] * 2 + [VMEM, HBM, VMEM, HBM, VMEM],
        [
            pltpu.VMEM((c_n * tokens, width), F32),
            pltpu.VMEM((c_n, c_n * tokens, half), BF),
            pltpu.VMEM((units, LANES), BF),
            pltpu.VMEM((c_n * tokens, width), BF),
            pltpu.SemaphoreType.DMA((2,)),
        ],
    )(core, high, both, target, weight[:, : width - LANES], pltpu.with_memory_space_constraint(weight, pltpu.HBM), bias[None, :])

    part = lax.all_to_all(part, ("y", "x"), 0, 0, tiled=True)
    spots = h_n * l_n
    part = call(
        functools.partial(plane_kernel, dims),
        shape((spots * TAIL, LANES), BF),
        [VMEM],
        [pltpu.VMEM((spots * TAIL, LANES), F32)],
    )(part)
    part, back = lax.optimization_barrier((part, back))
    part = lax.all_to_all(part.reshape(spots, TAIL, LANES), ("h", "l"), 0, 0, tiled=True)
    part = call(functools.partial(line_kernel, lines), shape((near, TAIL, LANES), BF), [VMEM] * 2)(part, back)
    part = lax.all_to_all(part, ("x", "l"), 0, 0, tiled=True).reshape(near * TAIL, LANES)
    wide = lax.all_gather(part, "c", axis=0, tiled=True)
    cos_sim, weight_grad, bias_grad = call(
        functools.partial(unpack_kernel, dims),
        (
            shape((1, tokens), F32),
            shape((units // (y_n * h_n), width), F32),
            shape((1, width // (y_n * h_n)), F32),
        ),
        [VMEM] * 4,
        [pltpu.VMEM((c_n * near * TAIL, LANES), F32), pltpu.VMEM((near * TAIL, LANES), F32)],
    )(back, part, wide, order)
    return cos_sim, weight_grad, bias_grad[0]


def solution(mesh, sizes=(4, 4, 4, 8, 2)):
    fine = Mesh(mesh.devices.reshape(sizes), ("y", "h", "x", "l", "c"))
    clip, seq = ("y", "h"), ("x", "l", "c")
    placed = (
        P(clip, seq, None),
        P(),
        P(),
        P(clip, seq, None),
        P(clip, seq),
        P(clip, seq),
        P(clip, seq),
    )
    return jax.shard_map(
        local,
        mesh=fine,
        in_specs=placed,
        out_specs=(P(clip, seq), P(clip, None), P(clip)),
        check_vma=False,
    )
```
